32 devices in a mesh: ep: 16 (over z, y, core), tp: 2 (over x).
Axes of the slice: x: 2, y: 2, z: 4, core: 2. Of those that a mesh axis runs over, the one named last changes fastest.
Arguments:
- grad_out: bfloat16 [2048, 3584], P('ep', 'tp'), may hold values from -6 to 6
- routes: int32 [2048, 8], P('ep'), may hold values from 0 to 15, all different within a row; in each aligned block of 128 rows (0 to 127, 128 to 255, ...) at most 66 rows name the same one
- gate_weights: float32 [2048, 8], P('ep'), may hold values from 0.05 to 0.5
- gate_act: bfloat16 [16, 1056, 1024], P('ep', None, 'tp'), may hold values from -6 to 6
- w_down: bfloat16 [16, 1024, 3584], P('ep', None, 'tp'), may hold values from -0.1875 to 0.1875
- w_up: bfloat16 [16, 3584, 1024], P('ep', 'tp'), may hold values from -0.09375 to 0.09375
Outputs:
- grad_in: bfloat16 [2048, 3584], P('ep', 'tp')
The draws below stay inside these ranges and needn't reach their ends.
Inputs may be any that keep to these rules, and one draw needn't show every extreme that they name: `routes`: each row names 8 different experts; among the 128 rows of one device no expert is named more than 66 times, a bound that some block reaches.
All inputs are finite; a program needn't handle non-finite values.
Results may differ from the reference program's by a relative error of at most 0.02.
Values may be sent and summed in bfloat16 or wider, within the bound.
No kernel may reach another device: no remote copies, remote signals or barrier semaphores. Data moves between devices by JAX's collectives and lax.ppermute only.
A program may use at most 64 MiB of HBM per device.

```python
import math
import jax
import jax.numpy as jnp
import numpy as np
from jax import lax

D = 3584
F = 1024
TOP = 8
TOK_DEV = 128
EXPERTS = 16
SLOT = 66
ROWS = 1056
TOKENS = 2048
N_EP = 16
N_TP = 2


def levels(rng, dims, pieces, smallest, high):
    level, own = 1.0, jax.random.fold_in(rng, 6)
    for dim, shards_of in pieces:
        heights = jnp.exp(jax.random.uniform(jax.random.fold_in(own, dim), (shards_of,), jnp.float32, smallest / len(pieces), high / len(pieces)))
        level = level * jnp.repeat(heights, dims[dim] // shards_of).reshape([-1 if axis == dim else 1 for axis in range(len(dims))])
    return level


def deal_out(own_key, own, number, rows, amount, top, limit, skew):
    ranking = jax.random.permutation(own_key, amount)
    packed, common = portions_of(amount, rows * top, limit, skew, True), portions_of(amount, rows * top, limit, skew, False)
    places = jnp.arange(amount)

    def named(tallies, offset_by):
        used = int((tallies > 0).sum())
        fixed = max(1, used // 4)
        passed = fixed + (places - fixed + offset_by * (used - fixed)) % max(1, amount - fixed)
        return jnp.zeros((amount,), jnp.int32).at[ranking[jnp.where(places < fixed, places, passed)]].set(jnp.asarray(tallies, jnp.int32))

    tallies = jnp.where(number % 4 == 0, named(packed, number // 4), named(common, number - number // 4 - 1))
    mixed = jax.random.permutation(jax.random.fold_in(own, 3), amount)
    source_of, receiver = mixed[0:amount // 2 * 2:2], mixed[1:amount // 2 * 2:2]
    slack = jnp.minimum(tallies[source_of] - 1, limit - tallies[receiver]) // 2
    slack = jnp.where((source_of == ranking[0]) | (receiver == ranking[0]) | (tallies[receiver] == 0), 0, jnp.maximum(slack, 0))
    passed = jax.random.randint(jax.random.fold_in(own, 4), (amount // 2,), 0, 1 << 20) % (slack + 1)
    tallies = tallies.at[source_of].add(-passed).at[receiver].add(passed)
    items = jnp.searchsorted(jnp.cumsum(tallies), jnp.arange(rows * top), side="right").astype(jnp.int32)
    table = items.reshape(top, rows).T
    table = table[jax.random.permutation(jax.random.fold_in(own, 1), rows)]
    offset_by = jax.random.randint(jax.random.fold_in(own, 2), (rows, 1), 0, top)
    return jnp.take_along_axis(table, (jnp.arange(top)[None, :] + offset_by) % top, axis=1)


def portions_of(count, total, limit, lean, full):
    portions = [(1 << 20) // math.isqrt(rank ** lean) + 1 for rank in range(1, count + 1)]
    largest = limit if full else min(limit, max(-(-total // count), total * portions[0] // sum(portions)))
    least = 1 if total - largest >= count - 1 else 0
    counts, spare = [largest] + [least] * (count - 1), total - largest - least * (count - 1)
    while spare > 0:
        movable = [i for i in range(1, count) if counts[i] < largest] or [i for i in range(1, count) if counts[i] < limit]
        pool, remaining = sum([portions[i] for i in movable]), spare
        for i in movable:
            more = min(limit - counts[i], max(1, remaining * portions[i] // pool), spare)
            counts[i] = counts[i] + more
            spare = spare - more
    return np.array(counts)


def centred(rng, shape, width, bound, shards=(), held_as=jnp.bfloat16):
    factor_of = levels(rng, shape, shards, -0.22, 0.18) if shards else 1.0
    values = jax.random.normal(rng, shape, jnp.float32) * width * factor_of
    return jnp.minimum(jnp.maximum(values, -bound), bound).astype(held_as)


def setup_inputs(seed: int = 0) -> dict:
    splits = jax.random.split(jax.random.key(seed), 7)
    grad_out = centred(splits[0], (TOKENS, D), 1.0, 6.0, ((0, 16), (1, 2)))
    routes_keys = jax.random.split(jax.random.fold_in(splits[1], 1), TOKENS // TOK_DEV)
    routes_turns = jax.random.permutation(jax.random.fold_in(splits[1], 3), TOKENS // TOK_DEV)
    routes = jax.vmap(lambda own, number: deal_out(jax.random.fold_in(splits[1], 2), own, number, TOK_DEV, EXPERTS, TOP, SLOT, 2))(routes_keys, routes_turns).reshape((TOKENS, TOP))
    gate_weights = jnp.clip(jnp.exp(math.log(0.5) - 2.3025851 * jax.random.uniform(splits[2], (TOKENS, TOP), jnp.float32) ** levels(splits[2], (TOKENS, TOP), ((0, 16),), -0.2, 0.2)), 0.05, 0.5)
    gate_act = centred(splits[3], (EXPERTS, ROWS, F), 1.0, 6.0, ((0, 16), (2, 2)))
    w_down = centred(splits[4], (EXPERTS, F, D), F ** -0.5, 0.1875, ((0, 16), (2, 2)))
    w_up = centred(splits[5], (EXPERTS, D, F), D ** -0.5, 0.09375, ((0, 16), (1, 2)))
    return {"grad_out": grad_out, "routes": routes, "gate_weights": gate_weights, "gate_act": gate_act, "w_down": w_down, "w_up": w_up}


def reference(grad_out, routes, gate_weights, gate_act, w_down, w_up):
    source_dev = (jnp.arange(TOKENS, dtype=jnp.int32) // TOK_DEV).astype(jnp.int32)
    flat_ids = routes.reshape(N_EP, TOK_DEV * TOP)
    one_hot = (flat_ids[:, :, None] == jnp.arange(EXPERTS, dtype=jnp.int32)[None, None, :]).astype(jnp.int32)
    earlier = jnp.cumsum(one_hot, axis=1) - one_hot
    slot_rank = jnp.sum(earlier * one_hot, axis=2).reshape(TOKENS, TOP).astype(jnp.int32)
    position = (routes * ROWS + source_dev[:, None] * SLOT + slot_rank).astype(jnp.int32).reshape(-1)
    token_ids = jnp.repeat(jnp.arange(TOKENS, dtype=jnp.int32), TOP)
    token_of = jnp.full((EXPERTS * ROWS,), TOKENS, jnp.int32).at[position].set(token_ids)
    weight_of = jnp.zeros((EXPERTS * ROWS,), jnp.float32).at[position].set(gate_weights.reshape(-1).astype(jnp.float32))
    padded = jnp.concatenate([grad_out, jnp.zeros((1, D), grad_out.dtype)], axis=0)
    token_of = token_of.reshape(EXPERTS, ROWS)
    weight_of = weight_of.reshape(EXPERTS, ROWS)
    quarter = D // N_TP

    def one_expert(accum, inputs):
        token_row, weight_row, act_row, down_mat, up_mat = inputs
        routed = (padded[token_row].astype(jnp.float32) * weight_row[:, None]).astype(jnp.bfloat16)
        hidden_grad = jnp.zeros((ROWS, F), jnp.float32)
        for part in range(N_TP):
            lower = part * quarter
            term = jnp.dot(routed[:, lower:lower + quarter], down_mat[:, lower:lower + quarter].T, preferred_element_type=jnp.float32)
            hidden_grad = hidden_grad + term.astype(jnp.bfloat16).astype(jnp.float32)
        up_grad = (hidden_grad * act_row.astype(jnp.float32)).astype(jnp.bfloat16)
        row_grad = jnp.dot(up_grad, up_mat.T, preferred_element_type=jnp.float32).astype(jnp.bfloat16)
        accum = accum.at[token_row].add(row_grad.astype(jnp.float32))
        return accum, None

    start = jnp.zeros((TOKENS + 1, D), jnp.float32)
    accum, _ = lax.scan(one_expert, start, (token_of, weight_of, gate_act, w_down, w_up))
    return accum[:TOKENS].astype(jnp.bfloat16)
```

```python
import functools

import jax
import jax.numpy as jnp
from jax import lax
from jax.experimental import pallas as pl
from jax.experimental.pallas import tpu as pltpu
from jax.sharding import PartitionSpec as P

BF16 = jnp.bfloat16
F32 = jnp.float32
VMEM = pl.BlockSpec(memory_space=pltpu.VMEM)
SMEM = pl.BlockSpec(memory_space=pltpu.SMEM)
LIMIT = pltpu.CompilerParams(vmem_limit_bytes=40 * 1024 * 1024)


def dot_t(a, b):
    return lax.dot_general(a, b, (((1,), (1,)), ((), ())), preferred_element_type=F32)


def meta_kernel(routes_ref, gates_ref, meta_ref):
    token_n, choose_n = routes_ref.shape
    expert_n = meta_ref.shape[0]
    wide = 128
    lane = lax.broadcasted_iota(jnp.int32, (token_n, wide), 1)
    chosen = jnp.zeros((token_n, wide), F32)
    weight = jnp.zeros((token_n, wide), F32)
    for k in range(choose_n):
        hit = routes_ref[:, k : k + 1] == lane
        chosen = jnp.where(hit, 1.0, chosen)
        weight = jnp.where(hit, gates_ref[:, k : k + 1], weight)
    first = lax.broadcasted_iota(jnp.int32, (token_n, token_n), 0)
    second = lax.broadcasted_iota(jnp.int32, (token_n, token_n), 1)
    earlier = jnp.where(second < first, 1.0, 0.0).astype(BF16)
    rank = jnp.dot(earlier, chosen.astype(BF16), preferred_element_type=F32)
    slot = jnp.where(chosen > 0.5, rank, -1.0)
    slot_t = jnp.transpose(slot)
    weight_t = jnp.transpose(weight)
    meta_ref[...] = jnp.zeros_like(meta_ref)
    for e in range(expert_n):
        meta_ref[e, 0:1, :] = slot_t[e : e + 1, :]
        meta_ref[e, 1:2, :] = weight_t[e : e + 1, :]


def act_kernel(slot_n, pieces, where_ref, act_ref, *out_refs):
    rows_n = act_ref.shape[0]
    at = 0
    for out_ref, piece_n in zip(out_refs, pieces):
        part = piece_n * slot_n
        row = lax.broadcasted_iota(jnp.int32, (part, 1), 0)
        target = row + where_ref[at] * slot_n
        for b in range(1, piece_n):
            target = jnp.where(row >= b * slot_n, row + (where_ref[at + b] - b) * slot_n, target)
        column = lax.broadcasted_iota(jnp.int32, (part, rows_n), 1)
        select = jnp.where(column == target, 1.0, 0.0).astype(BF16)
        out_ref[...] = jnp.dot(select, act_ref[...], preferred_element_type=F32).astype(BF16)
        at += piece_n


def selector(slot_n, piece_n, first, where_ref, meta_ref):
    slots, weights = [], []
    for b in range(piece_n):
        source = where_ref[first + b]
        slot = meta_ref[source, 0:1, :]
        slots.append(jnp.where(slot >= 0.0, slot + float(b * slot_n), -1.0))
        weights.append(meta_ref[source, 1:2, :])
    slots = jnp.concatenate(slots, axis=1).astype(jnp.int32)
    weights = jnp.concatenate(weights, axis=1)
    row = lax.broadcasted_iota(jnp.int32, (piece_n * slot_n, slots.shape[1]), 0)
    hit = row == slots
    return hit, weights


def down_kernel(slot_n, piece_n, first, halves, where_ref, meta_ref, *refs):
    source_n = where_ref.shape[0] - 2
    core, side = where_ref[source_n], where_ref[source_n + 1]
    block_refs, (w_ref, keep_ref, give_ref, rows_ref) = refs[:-4], refs[-4:]
    hit, weights = selector(slot_n, piece_n, first, where_ref, meta_ref)
    weight = jnp.sum(jnp.where(hit, weights, 0.0), axis=1, keepdims=True)
    select = jnp.where(hit, 1.0, 0.0).astype(BF16)
    if halves:
        half = block_refs[0].shape[1]
        token_n = meta_ref.shape[2]
        turned = jnp.concatenate([select[:, token_n:], select[:, :token_n]], axis=1)
        for ref, chosen, place in ((block_refs[0], select, core), (block_refs[1], turned, 1 - core)):
            value = jnp.dot(chosen, ref[...], preferred_element_type=F32)
            at = pl.multiple_of(place * half, 128)
            rows_ref[:, pl.ds(at, half)] = (value * weight).astype(BF16)
    else:
        value, at = None, 0
        for ref in block_refs:
            part = ref.shape[0]
            term = jnp.dot(select[:, at : at + part], ref[...], preferred_element_type=F32)
            value = term if value is None else value + term
            at += part
        rows_ref[...] = (value * weight).astype(BF16)
    unit = keep_ref.shape[1]
    tile = 256
    for out_ref, place in ((give_ref, 1 - side), (keep_ref, side)):
        for t in range(unit // tile):
            at = pl.multiple_of(place * unit + t * tile, tile)
            out_ref[:, t * tile : (t + 1) * tile] = dot_t(
                rows_ref[...], w_ref[pl.ds(at, tile), :]
            ).astype(BF16)


def up_kernel(slot_n, piece_n, first, halves, where_ref, meta_ref, mine_ref, peer_ref, w_ref, *refs):
    source_n = where_ref.shape[0] - 2
    core, side = where_ref[source_n], where_ref[source_n + 1]
    hit, _ = selector(slot_n, piece_n, first, where_ref, meta_ref)
    select = jnp.where(hit, 1.0, 0.0).astype(BF16)
    unit = mine_ref.shape[1]
    token_n = meta_ref.shape[2]
    feat_n = w_ref.shape[0]
    tile = 256 if feat_n % 256 == 0 else 128
    mine_at = pl.multiple_of(side * unit, 128)
    peer_at = pl.multiple_of((1 - side) * unit, 128)

    def placed(at):
        row = dot_t(mine_ref[...], w_ref[pl.ds(at, tile), pl.ds(mine_at, unit)])
        row = row + dot_t(peer_ref[...], w_ref[pl.ds(at, tile), pl.ds(peer_at, unit)])
        return lax.dot_general(
            select, row.astype(BF16), (((0,), (0,)), ((), ())), preferred_element_type=F32
        ).astype(BF16)

    if halves:
        tile = 128
        keep_ref, give_ref = refs
        half = feat_n // 2
        for t in range(half // tile):
            value = placed(pl.multiple_of(core * half + t * tile, tile))
            keep_ref[:token_n, t * tile : (t + 1) * tile] = value[token_n:]
            keep_ref[token_n:, t * tile : (t + 1) * tile] = value[:token_n]
            value = placed(pl.multiple_of((1 - core) * half + t * tile, tile))
            give_ref[:, t * tile : (t + 1) * tile] = value
    else:
        for t in range(feat_n // tile):
            value = placed(t * tile)
            at = 0
            for ref in refs:
                part = ref.shape[0]
                ref[:, t * tile : (t + 1) * tile] = value[at : at + part]
                at += part


def join_kernel(where_ref, keep_ref, given_ref, half_ref, out_ref):
    source_n = where_ref.shape[0] - 2
    core = where_ref[source_n]
    half = half_ref.shape[1]
    mine = pl.multiple_of(core * half, 128)
    other = pl.multiple_of((1 - core) * half, 128)
    total = keep_ref[:, pl.ds(mine, half)].astype(F32) + given_ref[:, pl.ds(mine, half)].astype(F32)
    out_ref[:, pl.ds(mine, half)] = (total + half_ref[...].astype(F32)).astype(BF16)
    total = keep_ref[:, pl.ds(other, half)].astype(F32) + given_ref[:, pl.ds(other, half)].astype(F32)
    out_ref[:, pl.ds(other, half)] = total.astype(BF16)


def ring_on_device(grad_out, routes, gate_weights, gate_act, w_down, w_up):
    experts_n = lax.axis_size("ep")
    slot_n = gate_act.shape[1] // experts_n
    token_n = routes.shape[0]
    feat_n = grad_out.shape[1]
    unit_n = gate_act.shape[2]
    chips_n = experts_n // 2
    far = chips_n // 2
    order = [2 * i for i in range(far)] + [2 * i + 1 for i in reversed(range(far))]
    spot = [order.index(c) for c in range(chips_n)]
    across = [(0, 1), (1, 0)]
    swap = [(i, i ^ 1) for i in range(experts_n)]
    ring = [
        (i, 2 * order[(spot[i // 2] + 1 - 2 * (i % 2)) % chips_n] + i % 2) for i in range(experts_n)
    ]

    def to_core(x):
        return lax.ppermute(x, "ep", swap)

    def to_ring(x):
        return lax.ppermute(x, "ep", ring)

    def to_side(x):
        return lax.ppermute(x, "tp", across)

    me = lax.axis_index("ep")
    core, side = me % 2, lax.axis_index("tp")
    here = jnp.array(spot, jnp.int32)[me // 2]
    table = jnp.array(order, jnp.int32)

    def chip_at(distance):
        return table[(here + distance * (2 * core - 1)) % chips_n]

    sources = [me, me ^ 1]
    for k in range(1, far):
        mine, sib = chip_at(k), chip_at(-k)
        sources += [2 * mine + core, 2 * mine + 1 - core, 2 * sib + 1 - core, 2 * sib + core]
    mine = chip_at(far)
    sources += [2 * mine + core, 2 * mine + 1 - core]
    where = jnp.stack([s.astype(jnp.int32) for s in sources + [core, side]])
    pieces = [2] + [4] * (far - 1) + [2]
    firsts = [sum(pieces[:k]) for k in range(far + 1)]

    blocks = [[grad_out, to_core(grad_out)]]
    moving = jnp.concatenate(blocks[0], axis=0)
    for k in range(1, far):
        moving = to_ring(moving)
        blocks.append([moving, to_core(moving)])
    half = feat_n // 2
    moving = to_ring(lax.dynamic_slice_in_dim(moving, core * half, half, 1))
    blocks.append([moving, to_core(moving)])

    meta = pl.pallas_call(
        meta_kernel,
        out_shape=jax.ShapeDtypeStruct((experts_n, 8, token_n), F32),
        in_specs=[VMEM, VMEM],
        out_specs=VMEM,
        name="meta",
    )(routes, gate_weights)
    meta = lax.all_to_all(meta, "ep", split_axis=0, concat_axis=0, tiled=True)
    acts = pl.pallas_call(
        functools.partial(act_kernel, slot_n, pieces),
        out_shape=[jax.ShapeDtypeStruct((p * slot_n, unit_n), BF16) for p in pieces],
        in_specs=[SMEM, VMEM],
        out_specs=[VMEM] * len(pieces),
        compiler_params=LIMIT,
        name="act",
    )(where, gate_act[0])

    keeps, gives = [], []
    for k in range(far + 1):
        rows_n = pieces[k] * slot_n
        part = jax.ShapeDtypeStruct((rows_n, unit_n), BF16)
        keep, give = pl.pallas_call(
            functools.partial(down_kernel, slot_n, pieces[k], firsts[k], k == far),
            out_shape=[part, part],
            in_specs=[SMEM] + [VMEM] * (len(blocks[k]) + 2),
            out_specs=[VMEM, VMEM],
            scratch_shapes=[pltpu.VMEM((rows_n, feat_n), BF16)],
            compiler_params=LIMIT,
            cost_estimate=pl.CostEstimate(
                flops=2 * rows_n * feat_n * (2 * unit_n + 128 * pieces[k]),
                bytes_accessed=2 * feat_n * 2 * unit_n,
                transcendentals=0,
            ),
            name="down%d" % k,
        )(where, meta, *blocks[k], w_down[0])
        hidden = keep.astype(F32) + to_side(give).astype(F32)
        up = (hidden * acts[k].astype(F32)).astype(BF16)
        up_peer = to_side(up)
        if k == far:
            outs = [jax.ShapeDtypeStruct((2 * token_n, half), BF16)] * 2
        else:
            outs = [jax.ShapeDtypeStruct((pieces[k] // 2 * token_n, feat_n), BF16)] * 2
        given, kept = pl.pallas_call(
            functools.partial(up_kernel, slot_n, pieces[k], firsts[k], k == far),
            out_shape=outs,
            in_specs=[SMEM] + [VMEM] * 4,
            out_specs=[VMEM, VMEM],
            compiler_params=LIMIT,
            cost_estimate=pl.CostEstimate(
                flops=2 * rows_n * feat_n * (2 * unit_n + 128 * pieces[k]),
                bytes_accessed=2 * feat_n * 2 * unit_n,
                transcendentals=0,
            ),
            name="up%d" % k,
        )(where, meta, up, up_peer, w_up[0])
        if k == far:
            given, kept = kept, given
        keeps.append(kept)
        gives.append(given)

    total = (keeps[far].astype(F32) + to_core(gives[far]).astype(F32)).astype(BF16)
    came = to_ring(total)
    for k in range(far - 1, 0, -1):
        given = to_core(gives[k])
        if k == far - 1:
            total = pl.pallas_call(
                join_kernel,
                out_shape=jax.ShapeDtypeStruct((2 * token_n, feat_n), BF16),
                in_specs=[SMEM] + [VMEM] * 3,
                out_specs=VMEM,
                compiler_params=LIMIT,
                name="join",
            )(where, keeps[k], given, came)
        else:
            total = (keeps[k].astype(F32) + given.astype(F32) + came.astype(F32)).astype(BF16)
        came = to_ring(total)
    other = (came[:token_n].astype(F32) + keeps[0].astype(F32)).astype(BF16)
    mine = came[token_n:].astype(F32) + gives[0].astype(F32)
    return (mine + to_core(other).astype(F32)).astype(BF16)


def spread_on_device(grad_out, routes, gate_weights, gate_act, w_down, w_up):
    experts_n = lax.axis_size("ep")
    slot_n = gate_act.shape[1] // experts_n
    rows_n = experts_n * slot_n
    token_n, choose_n = routes.shape
    flat_ids = routes.reshape(-1)
    one_hot = (flat_ids[:, None] == jnp.arange(experts_n, dtype=jnp.int32)[None, :]).astype(
        jnp.int32
    )
    earlier = jnp.cumsum(one_hot, axis=0) - one_hot
    slot_rank = jnp.sum(earlier * one_hot, axis=1)
    position = flat_ids * slot_n + slot_rank
    token_ids = jnp.arange(token_n * choose_n, dtype=jnp.int32) // choose_n
    token_of = jnp.full((rows_n,), token_n, jnp.int32).at[position].set(token_ids)
    weight_of = jnp.zeros((rows_n,), jnp.float32).at[position].set(gate_weights.reshape(-1))
    down_local = w_down[0]
    up_local = w_up[0]
    feat_part = grad_out.shape[1]
    padded = jnp.concatenate([grad_out, jnp.zeros((1, feat_part), grad_out.dtype)], axis=0)
    placed = (padded[token_of].astype(jnp.float32) * weight_of[:, None]).astype(jnp.bfloat16)
    placed = placed.reshape(experts_n, slot_n, feat_part)
    partial_value = jnp.einsum(
        "nsd,fd->nsf",
        lax.all_to_all(placed, "ep", split_axis=0, concat_axis=0, tiled=True),
        down_local,
        preferred_element_type=jnp.float32,
    )
    partial_value = partial_value.reshape(rows_n, -1)
    hidden_grad = lax.psum_scatter(
        partial_value.astype(jnp.bfloat16), "tp", scatter_dimension=1, tiled=True
    ).astype(jnp.float32)
    up_grad = (hidden_grad * gate_act[0].astype(jnp.float32)).astype(jnp.bfloat16)
    row_grad = lax.dot_general(
        lax.all_gather(up_grad, "tp", axis=1, tiled=True),
        up_local,
        (((1,), (1,)), ((), ())),
        preferred_element_type=jnp.float32,
    )
    row_grad = row_grad.astype(jnp.bfloat16).reshape(experts_n, slot_n, -1)
    returned = lax.all_to_all(row_grad, "ep", split_axis=0, concat_axis=0, tiled=True)
    picked = returned.reshape(rows_n, -1)[position]
    summed = jnp.sum(picked.astype(jnp.float32).reshape(token_n, choose_n, -1), axis=1)
    return summed.astype(jnp.bfloat16)


def solution(mesh):
    placed = (
        P("ep", "tp"),
        P("ep", None),
        P("ep", None),
        P("ep", None, "tp"),
        P("ep", None, "tp"),
        P("ep", "tp", None),
    )

    def whole(grad_out, routes, *rest):
        ep, tp = mesh.shape["ep"], mesh.shape["tp"]
        dense = tp == 2 and ep % 4 == 0 and 8 <= ep <= 2 * routes.shape[1]
        dense = dense and routes.shape[0] == 128 * ep and grad_out.shape[1] % 512 == 0
        return jax.shard_map(
            ring_on_device if dense else spread_on_device,
            mesh=mesh,
            in_specs=placed,
            out_specs=P("ep", "tp"),
            check_vma=False,
        )(grad_out, routes, *rest)

    return whole
```

```python
import functools

import jax
import jax.numpy as jnp
from jax import lax
from jax.experimental import pallas as pl
from jax.experimental.pallas import tpu as pltpu
from jax.sharding import PartitionSpec as P

BF16 = jnp.bfloat16
F32 = jnp.float32
VMEM = pl.BlockSpec(memory_space=pltpu.VMEM)
HBM = pl.BlockSpec(memory_space=pltpu.HBM)
TABLE = 128
LIMIT = pltpu.CompilerParams(vmem_limit_bytes=16 * 1024 * 1024)


def dot_t(a, b):
    return lax.dot_general(a, b, (((1,), (1,)), ((), ())), preferred_element_type=F32)


def prepare_kernel(rows_hbm, routes_hbm, gates_hbm, block_ref, routes_ref, gates_ref, sems):
    token_n, feat_n = rows_hbm.shape
    copies = [
        pltpu.make_async_copy(routes_hbm, routes_ref, sems.at[0]),
        pltpu.make_async_copy(gates_hbm, gates_ref, sems.at[1]),
        pltpu.make_async_copy(rows_hbm, block_ref.at[:, pl.ds(0, feat_n)], sems.at[2]),
    ]
    for copy in copies:
        copy.start()
    copies[0].wait()
    copies[1].wait()
    choose_n = routes_ref.shape[0]
    expert_n = lax.axis_size("ep")
    expert = lax.broadcasted_iota(jnp.int32, (expert_n, token_n), 0)
    chosen = jnp.zeros((expert_n, token_n), F32)
    weight = jnp.zeros((expert_n, token_n), F32)
    for k in range(choose_n):
        hit = routes_ref[k : k + 1, :] == expert
        chosen = jnp.where(hit, 1.0, chosen)
        weight = jnp.where(hit, gates_ref[k : k + 1, :], weight)
    first = lax.broadcasted_iota(jnp.int32, (token_n, token_n), 0)
    second = lax.broadcasted_iota(jnp.int32, (token_n, token_n), 1)
    earlier = jnp.where(first < second, 1.0, 0.0).astype(BF16)
    rank = jnp.dot(chosen.astype(BF16), earlier, preferred_element_type=F32)
    slot = jnp.where(chosen > 0.5, rank, -1.0)
    high = weight.astype(BF16).astype(F32)
    parts = [slot, high, weight - high]
    rest = jnp.zeros((TABLE - len(parts) * expert_n, token_n), F32)
    block_ref[:, feat_n:] = jnp.transpose(jnp.concatenate(parts + [rest], axis=0)).astype(BF16)
    copies[2].wait()


class Ring:
    def __init__(self, experts_n, slot_n, token_n):
        self.slot_n = slot_n
        self.token_n = token_n
        self.experts_n = experts_n
        self.chips_n = experts_n // 2
        self.far = self.chips_n // 2
        self.arrivals = [(0, 0), (0, 1)]
        for k in range(1, self.far):
            self.arrivals += [(k, 0), (k, 1), (-k, 1), (-k, 0)]
        self.arrivals += [(self.far, 0), (self.far, 1)]
        self.pieces = [2] + [4] * (self.far - 1) + [2]
        self.firsts = [sum(self.pieces[:k]) for k in range(self.far + 1)]

    def tables(self, chunk, refs):
        out = [(ref, at) for ref in refs for at in range(0, ref.shape[0], self.token_n)]
        return out[: self.pieces[chunk]]

    def chip(self, spot):
        return 2 * spot if spot < self.far else 2 * (self.chips_n - 1 - spot) + 1

    def pairs(self):
        out = []
        for i in range(self.experts_n):
            z, y = i // 4, i // 2 % 2
            spot = self.chips_n - 1 - z if y else z
            out.append((i, 2 * self.chip((spot + 1 - 2 * (i % 2)) % self.chips_n) + i % 2))
        return out

    def sources(self, chunk):
        me = lax.axis_index("ep")
        core = lax.rem(me, 2)
        z, y = me // 4, lax.rem(me // 2, 2)
        here = jnp.where(y == 1, self.chips_n - 1 - z, z)
        first = self.firsts[chunk]
        out = []
        for steps, flip in self.arrivals[first : first + self.pieces[chunk]]:
            spot = lax.rem(here + steps * (2 * core - 1) + self.chips_n, self.chips_n)
            chip = jnp.where(spot < self.far, 2 * spot, 2 * (self.chips_n - 1 - spot) + 1)
            out.append(2 * chip + (1 - core if flip else core))
        return out


def act_kernel(ring, act_ref, *out_refs):
    rows_n, slot_n = act_ref.shape[0], ring.slot_n
    for chunk, out_ref in enumerate(out_refs):
        part = out_ref.shape[0]
        row = lax.broadcasted_iota(jnp.int32, (part, 1), 0)
        target = row
        for b, source in enumerate(ring.sources(chunk)):
            target = jnp.where(row >= b * slot_n, row + (source - b) * slot_n, target)
        column = lax.broadcasted_iota(jnp.int32, (part, rows_n), 1)
        select = jnp.where(column == target, 1.0, 0.0).astype(BF16)
        out_ref[...] = jnp.dot(select, act_ref[...], preferred_element_type=F32).astype(BF16)


def mine_of(*columns):
    me, expert_n = lax.axis_index("ep"), lax.axis_size("ep")
    row = lax.broadcasted_iota(jnp.int32, (8, TABLE), 0)
    lane = lax.broadcasted_iota(jnp.int32, (8, TABLE), 1)
    hit = row < 0
    for i, parts in enumerate(columns):
        for part in parts:
            hit = hit | ((row == i) & (lane == part * expert_n + me))
    return jnp.where(hit, 1.0, 0.0).astype(BF16)


def down_kernel(ring, chunk, *refs):
    core, side = lax.rem(lax.axis_index("ep"), 2), lax.axis_index("tp")
    whole = chunk == ring.far
    outs_n = 1 if whole else 2
    blocks, w_ref = refs[: -3 - outs_n], refs[-3 - outs_n]
    outs, table_ref, rows_ref = refs[-2 - outs_n : -2], refs[-2], refs[-1]
    slot_n, token_n = ring.slot_n, ring.token_n
    feat_n = w_ref.shape[1]
    mine = mine_of((0,), (1, 2))
    slots, weights = [], []
    for b, (ref, at) in enumerate(ring.tables(chunk, blocks)):
        table = ref[at : at + token_n, ref.shape[1] - TABLE :]
        table_ref[b * token_n : (b + 1) * token_n, :] = table
        table = dot_t(mine, table)
        slots.append(jnp.where(table[0:1] >= 0.0, table[0:1] + float(b * slot_n), -1.0))
        weights.append(table[1:2])
    slots = jnp.concatenate(slots, axis=1).astype(jnp.int32)
    weights = jnp.concatenate(weights, axis=1)
    hit = lax.broadcasted_iota(jnp.int32, (rows_ref.shape[0], slots.shape[1]), 0) == slots
    weight = jnp.sum(jnp.where(hit, weights, 0.0), axis=1, keepdims=True)
    select = jnp.where(hit, 1.0, 0.0).astype(BF16)

    def chosen(select, parts):
        value, at = None, 0
        for ref in parts:
            rows = ref[:, : ref.shape[1] - TABLE]
            term = jnp.dot(select[:, at : at + ref.shape[0]], rows, preferred_element_type=F32)
            value = term if value is None else value + term
            at += ref.shape[0]
        return (value * weight).astype(BF16)

    if whole:
        half = feat_n // 2
        turned = jnp.concatenate([select[:, token_n:], select[:, :token_n]], axis=1)
        rows_ref[:, pl.ds(pl.multiple_of(core * half, 128), half)] = chosen(select, blocks[:1])
        rows_ref[:, pl.ds(pl.multiple_of((1 - core) * half, 128), half)] = chosen(turned, blocks[1:])
    else:
        rows_ref[...] = chosen(select, blocks)
    tile = 256
    if whole:
        (out_ref,) = outs
        for at in range(0, out_ref.shape[1], tile):
            out_ref[:, at : at + tile] = dot_t(rows_ref[...], w_ref[at : at + tile, :]).astype(BF16)
    else:
        unit = outs[0].shape[1]
        for out_ref, place in zip(outs, (side, 1 - side)):
            for t in range(0, unit, tile):
                at = pl.multiple_of(place * unit + t, tile)
                out_ref[:, t : t + tile] = dot_t(rows_ref[...], w_ref[pl.ds(at, tile), :]).astype(BF16)


def up_kernel(ring, chunk, *refs):
    if chunk == ring.far:
        refs, all_ref = refs[:-1], refs[-1]
    core, side = lax.rem(lax.axis_index("ep"), 2), lax.axis_index("tp")
    table_ref, ins, (w_ref, keep_ref, give_ref) = refs[0], refs[1:-3], refs[-3:]
    slot_n, token_n = ring.slot_n, ring.token_n
    feat_n, unit = w_ref.shape[0], w_ref.shape[1] // 2
    mine_at = pl.multiple_of(side * unit, 128)
    peer_at = pl.multiple_of((1 - side) * unit, 128)
    if len(ins) == 2:
        ups = [ref[...] for ref in ins]
    else:
        ups = []
        for at, act_ref in ((mine_at, ins[2]), (peer_at, ins[3])):
            hidden = ins[0][:, pl.ds(at, unit)].astype(F32) + ins[1][:, pl.ds(at, unit)].astype(F32)
            ups.append((hidden * act_ref[...].astype(F32)).astype(BF16))
    rows_n = ups[0].shape[0]
    window = rows_n if rows_n <= 2 * slot_n else 2 * slot_n + (-2 * slot_n) % 16
    lane = lax.broadcasted_iota(jnp.int32, (token_n, window), 1)
    mine = mine_of((0,))
    selects, starts = [], []
    for b, (ref, at) in enumerate(ring.tables(chunk, [table_ref])):
        start = 0 if b < 2 else rows_n - window
        slot = dot_t(ref[at : at + token_n, :], mine)[:, 0:1].astype(jnp.int32)
        slot = jnp.where(slot >= 0, slot + (b * slot_n - start), -1)
        selects.append(jnp.where(lane == slot, 1.0, 0.0).astype(BF16))
        starts.append(start)
    selects = [jnp.concatenate(selects[b : b + 2], axis=0) for b in range(0, len(selects), 2)]

    def placed(at, tile):
        row = dot_t(ups[0], w_ref[pl.ds(at, tile), pl.ds(mine_at, unit)])
        row = row + dot_t(ups[1], w_ref[pl.ds(at, tile), pl.ds(peer_at, unit)])
        row = row.astype(BF16)
        out = []
        for select, start in zip(selects, starts[::2]):
            part = row[start : start + window]
            out.append(jnp.dot(select, part, preferred_element_type=F32).astype(BF16))
        return out

    tile = 256
    if chunk == ring.far:
        half = feat_n // 2
        for t in range(0, feat_n, tile):
            (value,) = placed(t, tile)
            all_ref[:, t : t + tile] = value
        keep = pl.ds(pl.multiple_of(core * half, 128), half)
        keep_ref[:token_n, :] = all_ref[token_n:, keep]
        keep_ref[token_n:, :] = all_ref[:token_n, keep]
        give_ref[...] = all_ref[:, pl.ds(pl.multiple_of((1 - core) * half, 128), half)]
    else:
        for t in range(0, feat_n, tile):
            value = placed(t, tile)
            if chunk == 0:
                value = [value[0][:token_n], value[0][token_n:]]
            give_ref[:, t : t + tile] = value[0]
            keep_ref[:, t : t + tile] = value[1]


def join_kernel(first, keep_ref, *refs):
    core = lax.rem(lax.axis_index("ep"), 2)
    given_refs, came_ref, out_ref = refs[:-2], refs[-2], refs[-1]
    feat_n, half = out_ref.shape[1], came_ref.shape[1]
    at = 0
    for given_ref in given_refs:
        rows = pl.ds(at, given_ref.shape[0])
        kept = pl.ds(first + at, given_ref.shape[0])

        def total(columns):
            return keep_ref[kept, columns].astype(F32) + given_ref[:, columns].astype(F32)

        if half == feat_n:
            value = total(pl.ds(0, feat_n)) + came_ref[rows, :].astype(F32)
            out_ref[rows, :] = value.astype(BF16)
        else:
            mine = pl.ds(pl.multiple_of(core * half, 128), half)
            other = pl.ds(pl.multiple_of((1 - core) * half, 128), half)
            out_ref[rows, mine] = (total(mine) + came_ref[rows, :].astype(F32)).astype(BF16)
            out_ref[rows, other] = total(other).astype(BF16)
        at += given_ref.shape[0]


def after(value, *others):
    return lax.optimization_barrier((value, *others))[0]


def ring_on_device(grad_out, routes, gate_weights, gate_act, w_down, w_up):
    experts_n = lax.axis_size("ep")
    slot_n = gate_act.shape[1] // experts_n
    token_n = routes.shape[0]
    feat_n = grad_out.shape[1]
    half = feat_n // 2
    unit_n = gate_act.shape[2]
    ring = Ring(experts_n, slot_n, token_n)
    far, pieces = ring.far, ring.pieces
    swap = [(i, i ^ 1) for i in range(experts_n)]
    ring_pairs = ring.pairs()
    core = lax.axis_index("ep") % 2

    def parts_to_core(x, rows):
        return [lax.ppermute(p, "ep", swap) for p in jnp.split(x, x.shape[0] // rows)]

    def to_core(x, rows=128):
        return jnp.concatenate(parts_to_core(x, rows), axis=0)

    def to_ring(x):
        return lax.ppermute(x, "ep", ring_pairs)

    def to_side(x):
        return lax.ppermute(x, "tp", [(0, 1), (1, 0)])

    def call(kernel, outs, *args, scratch=()):
        return pl.pallas_call(
            kernel,
            out_shape=[jax.ShapeDtypeStruct(shape, BF16) for shape in outs],
            in_specs=[VMEM] * len(args),
            out_specs=[VMEM] * len(outs),
            scratch_shapes=scratch,
            compiler_params=LIMIT,
        )(*args)

    def down(k):
        rows_n = pieces[k] * slot_n
        return call(
            functools.partial(down_kernel, ring, k),
            ([(rows_n, 2 * unit_n)] if k == far else [(rows_n, unit_n)] * 2)
            + [(pieces[k] * token_n, TABLE)],
            *blocks[k],
            w_down[0],
            scratch=[pltpu.VMEM((rows_n, feat_n), BF16)],
        )

    def middle(k, sent):
        hidden = partials[k][0].astype(F32) + sent.astype(F32)
        return (hidden * acts[k].astype(F32)).astype(BF16)

    def up(k, *args):
        shape = (2 * token_n, half) if k == far else (pieces[k] // 2 * token_n, feat_n)
        return call(
            functools.partial(up_kernel, ring, k),
            [shape] * 2,
            partials[k][-1],
            *args,
            w_up[0],
            scratch=[pltpu.VMEM((2 * token_n, feat_n), BF16)] if k == far else [],
        )

    def join(first, width, *args):
        return call(functools.partial(join_kernel, first), [(token_n, width)], *args)[0]

    own = pl.pallas_call(
        prepare_kernel,
        out_shape=jax.ShapeDtypeStruct((token_n, feat_n + TABLE), BF16),
        in_specs=[HBM] * 3,
        out_specs=VMEM,
        scratch_shapes=[
            pltpu.VMEM(routes.shape[::-1], jnp.int32),
            pltpu.VMEM(routes.shape[::-1], F32),
            pltpu.SemaphoreType.DMA((3,)),
        ],
        compiler_params=LIMIT,
    )(grad_out, routes.T, gate_weights.T)
    sibling = to_core(own)
    blocks = [[own, sibling]]
    moving = to_ring(jnp.concatenate(blocks[0], axis=0))
    acts = call(
        functools.partial(act_kernel, ring),
        [(p * slot_n, unit_n) for p in pieces],
        gate_act[0],
    )
    act_peer = to_side(acts[far])
    partials, mines, peers, ups = [down(0)], {}, {}, {}
    sents = [to_side(partials[0][1])]
    for k in range(1, far + 1):
        ended = [partials[k - 1][0]]
        if k < far:
            ended += [sents[k - 1]] + ([act_peer] if k == 1 else [])
        if k >= 3:
            ended += [peers[k - 2]]
        here = after(moving, *ended)
        if k < far - 1:
            moving = to_ring(here)
        elif k == far - 1:
            part = lax.dynamic_slice_in_dim(here, core * half, half, 1)
            moving = to_ring(jnp.concatenate([part, here[:, feat_n:]], axis=1))
        if 2 <= k < far:
            mines[k - 1] = middle(k - 1, after(sents[k - 1], here))
            peers[k - 1] = to_side(mines[k - 1])
            here = after(here, mines[k - 1])
        blocks.append([here, to_core(here, 64 if k == far else 128)])
        if k == far:
            mines[k - 1] = middle(k - 1, sents[k - 1])
            blocks[k][1] = after(blocks[k][1], mines[k - 1])
        partials.append(down(k))
        sents.append(to_side(partials[k][-2]))

    for k in range(1, far - 1):
        ups[k] = up(k, mines[k], after(peers[k], partials[far][0]))
    full = after(sents[far], *(ups[k][0] for k in range(1, far - 1)))
    ups[far] = up(far, partials[far][0], full, acts[far], act_peer)
    peer = to_side(after(mines[far - 1], full))
    keep, give = ups[far]
    total = (keep.astype(F32) + to_core(give, 64).astype(F32)).astype(BF16)
    came = to_ring(total)
    ups[far - 1] = up(far - 1, mines[far - 1], after(peer, total))
    mines[0] = middle(0, after(sents[0], peer))
    peer = to_side(mines[0])
    came = [came[:token_n], came[token_n:]]
    for k in range(far - 1, 0, -1):
        keep, give = ups[k]
        rows = 64 if k == far - 1 else 128
        given = parts_to_core(give, rows)
        for i in range(2):
            parts = given[i * (token_n // rows) : (i + 1) * (token_n // rows)]
            total = join(i * token_n, feat_n, keep, *parts, came[i])
            came[i] = to_ring(total)
        came[0] = after(came[0], total)
    keep, give = up(0, mines[0], after(peer, total))
    total = to_core((came[0].astype(F32) + keep.astype(F32)).astype(BF16))
    return (came[1].astype(F32) + give.astype(F32) + total.astype(F32)).astype(BF16)


def spread_on_device(grad_out, routes, gate_weights, gate_act, w_down, w_up):
    experts_n = lax.axis_size("ep")
    slot_n = gate_act.shape[1] // experts_n
    rows_n = experts_n * slot_n
    token_n, choose_n = routes.shape
    flat_ids = routes.reshape(-1)
    one_hot = (flat_ids[:, None] == jnp.arange(experts_n, dtype=jnp.int32)[None, :]).astype(
        jnp.int32
    )
    earlier = jnp.cumsum(one_hot, axis=0) - one_hot
    slot_rank = jnp.sum(earlier * one_hot, axis=1)
    position = flat_ids * slot_n + slot_rank
    token_ids = jnp.arange(token_n * choose_n, dtype=jnp.int32) // choose_n
    token_of = jnp.full((rows_n,), token_n, jnp.int32).at[position].set(token_ids)
    weight_of = jnp.zeros((rows_n,), jnp.float32).at[position].set(gate_weights.reshape(-1))
    down_local = w_down[0]
    up_local = w_up[0]
    feat_part = grad_out.shape[1]
    padded = jnp.concatenate([grad_out, jnp.zeros((1, feat_part), grad_out.dtype)], axis=0)
    placed = (padded[token_of].astype(jnp.float32) * weight_of[:, None]).astype(jnp.bfloat16)
    placed = placed.reshape(experts_n, slot_n, feat_part)
    partial_value = jnp.einsum(
        "nsd,fd->nsf",
        lax.all_to_all(placed, "ep", split_axis=0, concat_axis=0, tiled=True),
        down_local,
        preferred_element_type=jnp.float32,
    )
    partial_value = partial_value.reshape(rows_n, -1)
    hidden_grad = lax.psum_scatter(
        partial_value.astype(jnp.bfloat16), "tp", scatter_dimension=1, tiled=True
    ).astype(jnp.float32)
    up_grad = (hidden_grad * gate_act[0].astype(jnp.float32)).astype(jnp.bfloat16)
    row_grad = lax.dot_general(
        lax.all_gather(up_grad, "tp", axis=1, tiled=True),
        up_local,
        (((1,), (1,)), ((), ())),
        preferred_element_type=jnp.float32,
    )
    row_grad = row_grad.astype(jnp.bfloat16).reshape(experts_n, slot_n, -1)
    returned = lax.all_to_all(row_grad, "ep", split_axis=0, concat_axis=0, tiled=True)
    picked = returned.reshape(rows_n, -1)[position]
    summed = jnp.sum(picked.astype(jnp.float32).reshape(token_n, choose_n, -1), axis=1)
    return summed.astype(jnp.bfloat16)


def solution(mesh):
    placed = (
        P("ep", "tp"),
        P("ep", None),
        P("ep", None),
        P("ep", None, "tp"),
        P("ep", None, "tp"),
        P("ep", "tp", None),
    )

    def whole(grad_out, routes, *rest):
        ep, tp = mesh.shape["ep"], mesh.shape["tp"]
        dense = tp == 2 and ep % 4 == 0 and 8 <= ep <= 2 * routes.shape[1]
        dense = dense and routes.shape[0] == 128 * ep and grad_out.shape[1] % 512 == 0
        return jax.shard_map(
            ring_on_device if dense else spread_on_device,
            mesh=mesh,
            in_specs=placed,
            out_specs=P("ep", "tp"),
            check_vma=False,
        )(grad_out, routes, *rest)

    return whole
```

```python
import functools

import jax
import jax.numpy as jnp
from jax import lax
from jax.experimental import pallas as pl
from jax.experimental.pallas import tpu as pltpu
from jax.sharding import PartitionSpec as P

BF16 = jnp.bfloat16
F32 = jnp.float32
VMEM = pl.BlockSpec(memory_space=pltpu.VMEM)
HBM = pl.BlockSpec(memory_space=pltpu.HBM)
TABLE = 128
LIMIT = pltpu.CompilerParams(vmem_limit_bytes=16 * 1024 * 1024)


def dot_t(a, b):
    return lax.dot_general(a, b, (((1,), (1,)), ((), ())), preferred_element_type=F32)


def prepare_kernel(rows_hbm, routes_hbm, gates_hbm, block_ref, routes_ref, gates_ref, sems):
    token_n, feat_n = rows_hbm.shape
    copies = [
        pltpu.make_async_copy(routes_hbm, routes_ref, sems.at[0]),
        pltpu.make_async_copy(gates_hbm, gates_ref, sems.at[1]),
        pltpu.make_async_copy(rows_hbm, block_ref.at[:, pl.ds(0, feat_n)], sems.at[2]),
    ]
    for copy in copies:
        copy.start()
    copies[0].wait()
    copies[1].wait()
    choose_n = routes_ref.shape[0]
    expert_n = lax.axis_size("ep")
    expert = lax.broadcasted_iota(jnp.int32, (expert_n, token_n), 0)
    chosen = jnp.zeros((expert_n, token_n), F32)
    weight = jnp.zeros((expert_n, token_n), F32)
    for k in range(choose_n):
        hit = routes_ref[k : k + 1, :] == expert
        chosen = jnp.where(hit, 1.0, chosen)
        weight = jnp.where(hit, gates_ref[k : k + 1, :], weight)
    first = lax.broadcasted_iota(jnp.int32, (token_n, token_n), 0)
    second = lax.broadcasted_iota(jnp.int32, (token_n, token_n), 1)
    earlier = jnp.where(first < second, 1.0, 0.0).astype(BF16)
    rank = jnp.dot(chosen.astype(BF16), earlier, preferred_element_type=F32)
    slot = jnp.where(chosen > 0.5, rank, -1.0)
    high = weight.astype(BF16).astype(F32)
    parts = [slot, high, weight - high]
    rest = jnp.zeros((TABLE - len(parts) * expert_n, token_n), F32)
    block_ref[:, feat_n:] = jnp.transpose(jnp.concatenate(parts + [rest], axis=0)).astype(BF16)
    copies[2].wait()


class Ring:
    def __init__(self, experts_n, slot_n, token_n):
        self.slot_n = slot_n
        self.token_n = token_n
        self.experts_n = experts_n
        self.chips_n = experts_n // 2
        self.far = self.chips_n // 2
        self.arrivals = [(0, 0), (0, 1)]
        for k in range(1, self.far):
            self.arrivals += [(k, 0), (k, 1), (-k, 1), (-k, 0)]
        self.arrivals += [(self.far, 0), (self.far, 1)]
        self.pieces = [2] + [4] * (self.far - 1) + [2]
        self.firsts = [sum(self.pieces[:k]) for k in range(self.far + 1)]

    def tables(self, chunk, refs):
        out = [(ref, at) for ref in refs for at in range(0, ref.shape[0], self.token_n)]
        return out[: self.pieces[chunk]]

    def chip(self, spot):
        return 2 * spot if spot < self.far else 2 * (self.chips_n - 1 - spot) + 1

    def pairs(self):
        out = []
        for i in range(self.experts_n):
            z, y = i // 4, i // 2 % 2
            spot = self.chips_n - 1 - z if y else z
            out.append((i, 2 * self.chip((spot + 1 - 2 * (i % 2)) % self.chips_n) + i % 2))
        return out

    def sources(self, chunk):
        me = lax.axis_index("ep")
        core = lax.rem(me, 2)
        z, y = me // 4, lax.rem(me // 2, 2)
        here = jnp.where(y == 1, self.chips_n - 1 - z, z)
        first = self.firsts[chunk]
        out = []
        for steps, flip in self.arrivals[first : first + self.pieces[chunk]]:
            spot = lax.rem(here + steps * (2 * core - 1) + self.chips_n, self.chips_n)
            chip = jnp.where(spot < self.far, 2 * spot, 2 * (self.chips_n - 1 - spot) + 1)
            out.append(2 * chip + (1 - core if flip else core))
        return out


def act_kernel(ring, act_ref, *out_refs):
    rows_n, slot_n = act_ref.shape[0], ring.slot_n
    for chunk, out_ref in enumerate(out_refs):
        part = out_ref.shape[0]
        row = lax.broadcasted_iota(jnp.int32, (part, 1), 0)
        target = row
        for b, source in enumerate(ring.sources(chunk)):
            target = jnp.where(row >= b * slot_n, row + (source - b) * slot_n, target)
        column = lax.broadcasted_iota(jnp.int32, (part, rows_n), 1)
        select = jnp.where(column == target, 1.0, 0.0).astype(BF16)
        out_ref[...] = jnp.dot(select, act_ref[...], preferred_element_type=F32).astype(BF16)


def mine_of(*columns):
    me, expert_n = lax.axis_index("ep"), lax.axis_size("ep")
    row = lax.broadcasted_iota(jnp.int32, (8, TABLE), 0)
    lane = lax.broadcasted_iota(jnp.int32, (8, TABLE), 1)
    hit = row < 0
    for i, parts in enumerate(columns):
        for part in parts:
            hit = hit | ((row == i) & (lane == part * expert_n + me))
    return jnp.where(hit, 1.0, 0.0).astype(BF16)


def down_kernel(ring, chunk, *refs):
    core, side = lax.rem(lax.axis_index("ep"), 2), lax.axis_index("tp")
    whole = chunk == ring.far
    outs_n = 1 if whole else 2
    blocks, w_ref = refs[: -3 - outs_n], refs[-3 - outs_n]
    outs, table_ref, rows_ref = refs[-2 - outs_n : -2], refs[-2], refs[-1]
    slot_n, token_n = ring.slot_n, ring.token_n
    feat_n = w_ref.shape[1]
    mine = mine_of((0,), (1, 2))
    slots, weights = [], []
    for b, (ref, at) in enumerate(ring.tables(chunk, blocks)):
        table = ref[at : at + token_n, ref.shape[1] - TABLE :]
        table_ref[b * token_n : (b + 1) * token_n, :] = table
        table = dot_t(mine, table)
        slots.append(jnp.where(table[0:1] >= 0.0, table[0:1] + float(b * slot_n), -1.0))
        weights.append(table[1:2])
    slots = jnp.concatenate(slots, axis=1).astype(jnp.int32)
    weights = jnp.concatenate(weights, axis=1)
    hit = lax.broadcasted_iota(jnp.int32, (rows_ref.shape[0], slots.shape[1]), 0) == slots
    weight = jnp.sum(jnp.where(hit, weights, 0.0), axis=1, keepdims=True)
    select = jnp.where(hit, 1.0, 0.0).astype(BF16)

    def chosen(select, parts):
        value, at = None, 0
        for ref in parts:
            rows = ref[:, : ref.shape[1] - TABLE]
            term = jnp.dot(select[:, at : at + ref.shape[0]], rows, preferred_element_type=F32)
            value = term if value is None else value + term
            at += ref.shape[0]
        return (value * weight).astype(BF16)

    if whole:
        half = feat_n // 2
        turned = jnp.concatenate([select[:, token_n:], select[:, :token_n]], axis=1)
        rows_ref[:, pl.ds(pl.multiple_of(core * half, 128), half)] = chosen(select, blocks[:1])
        rows_ref[:, pl.ds(pl.multiple_of((1 - core) * half, 128), half)] = chosen(turned, blocks[1:])
    else:
        rows_ref[...] = chosen(select, blocks)
    tile = 256
    if whole:
        (out_ref,) = outs
        for at in range(0, out_ref.shape[1], tile):
            out_ref[:, at : at + tile] = dot_t(rows_ref[...], w_ref[at : at + tile, :]).astype(BF16)
    else:
        unit = outs[0].shape[1]
        for out_ref, place in zip(outs, (side, 1 - side)):
            for t in range(0, unit, tile):
                at = pl.multiple_of(place * unit + t, tile)
                out_ref[:, t : t + tile] = dot_t(rows_ref[...], w_ref[pl.ds(at, tile), :]).astype(BF16)


def up_kernel(ring, chunk, table_ref, *refs):
    core, side = lax.rem(lax.axis_index("ep"), 2), lax.axis_index("tp")
    ins, (w_ref, keep_ref, give_ref, up_ref, row_ref) = refs[:-5], refs[-5:]
    slot_n, token_n = ring.slot_n, ring.token_n
    feat_n, unit = w_ref.shape[0], w_ref.shape[1] // 2
    mine_at = pl.multiple_of(side * unit, 128)
    peer_at = pl.multiple_of((1 - side) * unit, 128)
    if len(ins) == 2:
        up_ref[:, pl.ds(mine_at, unit)] = ins[0][...]
        up_ref[:, pl.ds(peer_at, unit)] = ins[1][...]
    else:
        for at, act_ref in ((mine_at, ins[2]), (peer_at, ins[3])):
            part = pl.ds(at, unit)
            hidden = ins[0][:, part].astype(F32) + ins[1][:, part].astype(F32)
            up_ref[:, part] = (hidden * act_ref[...].astype(F32)).astype(BF16)
    rows_n = up_ref.shape[0]
    tile = 256
    for t in range(0, feat_n, tile):
        row_ref[:, t : t + tile] = dot_t(up_ref[...], w_ref[t : t + tile, :]).astype(BF16)
    window = rows_n if rows_n <= 2 * slot_n else 2 * slot_n + (-2 * slot_n) % 16
    lane = lax.broadcasted_iota(jnp.int32, (token_n, window), 1)
    mine = mine_of((0,))
    selects, starts = [], []
    for b in range(ring.pieces[chunk]):
        start = 0 if b < 2 else rows_n - window
        table = table_ref[b * token_n : (b + 1) * token_n, :]
        slot = dot_t(table, mine)[:, 0:1].astype(jnp.int32)
        slot = jnp.where(slot >= 0, slot + (b * slot_n - start), -1)
        selects.append(jnp.where(lane == slot, 1.0, 0.0).astype(BF16))
        starts.append(start)

    def placed(b, sources_n, columns):
        select = jnp.concatenate(selects[b : b + sources_n], axis=0)
        rows = row_ref[starts[b] : starts[b] + window, columns]
        return jnp.dot(select, rows, preferred_element_type=F32).astype(BF16)

    if chunk == ring.far:
        half = feat_n // 2
        keep = placed(0, 2, pl.ds(pl.multiple_of(core * half, 128), half))
        keep_ref[:token_n, :] = keep[token_n:]
        keep_ref[token_n:, :] = keep[:token_n]
        give_ref[...] = placed(0, 2, pl.ds(pl.multiple_of((1 - core) * half, 128), half))
    else:
        sources_n = ring.pieces[chunk] // 2
        give_ref[...] = placed(0, sources_n, pl.ds(0, feat_n))
        keep_ref[...] = placed(sources_n, sources_n, pl.ds(0, feat_n))


def join_kernel(first, keep_ref, *refs):
    core = lax.rem(lax.axis_index("ep"), 2)
    out_ref = refs[-1]
    rows_n, feat_n = out_ref.shape
    given_refs, at = [], 0
    while at < rows_n:
        given_refs.append(refs[len(given_refs)])
        at += given_refs[-1].shape[0]
    came_refs = refs[len(given_refs) : -1]
    half = came_refs[0].shape[1] if came_refs else feat_n
    at = 0
    for given_ref in given_refs:
        rows = pl.ds(at, given_ref.shape[0])
        kept = pl.ds(first + at, given_ref.shape[0])

        def total(columns):
            return keep_ref[kept, columns].astype(F32) + given_ref[:, columns].astype(F32)

        if half == feat_n:
            value = total(pl.ds(0, feat_n))
            for came_ref in came_refs:
                value = value + came_ref[rows, :].astype(F32)
            out_ref[rows, :] = value.astype(BF16)
        else:
            mine = pl.ds(pl.multiple_of(core * half, 128), half)
            other = pl.ds(pl.multiple_of((1 - core) * half, 128), half)
            value = total(mine) + came_refs[0][rows, :].astype(F32)
            out_ref[rows, mine] = value.astype(BF16)
            out_ref[rows, other] = total(other).astype(BF16)
        at += given_ref.shape[0]


def after(value, *others):
    return lax.optimization_barrier((value, *others))[0]


def ring_on_device(grad_out, routes, gate_weights, gate_act, w_down, w_up):
    experts_n = lax.axis_size("ep")
    slot_n = gate_act.shape[1] // experts_n
    token_n = routes.shape[0]
    feat_n = grad_out.shape[1]
    half = feat_n // 2
    unit_n = gate_act.shape[2]
    ring = Ring(experts_n, slot_n, token_n)
    far, pieces = ring.far, ring.pieces
    swap = [(i, i ^ 1) for i in range(experts_n)]
    ring_pairs = ring.pairs()
    core = lax.axis_index("ep") % 2

    def parts_to_core(x, rows):
        return [lax.ppermute(p, "ep", swap) for p in jnp.split(x, x.shape[0] // rows)]

    def to_core(x, rows=128):
        return jnp.concatenate(parts_to_core(x, rows), axis=0)

    def to_ring(x):
        return lax.ppermute(x, "ep", ring_pairs)

    def to_side(x):
        return lax.ppermute(x, "tp", [(0, 1), (1, 0)])

    def call(kernel, outs, *args, scratch=()):
        return pl.pallas_call(
            kernel,
            out_shape=[jax.ShapeDtypeStruct(shape, BF16) for shape in outs],
            in_specs=[VMEM] * len(args),
            out_specs=[VMEM] * len(outs),
            scratch_shapes=scratch,
            compiler_params=LIMIT,
        )(*args)

    def down(k):
        rows_n = pieces[k] * slot_n
        return call(
            functools.partial(down_kernel, ring, k),
            ([(rows_n, 2 * unit_n)] if k == far else [(rows_n, unit_n)] * 2)
            + [(pieces[k] * token_n, TABLE)],
            *blocks[k],
            w_down[0],
            scratch=[pltpu.VMEM((rows_n, feat_n), BF16)],
        )

    def middle(k, sent):
        hidden = partials[k][0].astype(F32) + sent.astype(F32)
        return (hidden * acts[k].astype(F32)).astype(BF16)

    def up(k, *args):
        shape = (2 * token_n, half) if k == far else (pieces[k] // 2 * token_n, feat_n)
        return call(
            functools.partial(up_kernel, ring, k),
            [shape] * 2,
            partials[k][-1],
            *args,
            w_up[0],
            scratch=[pltpu.VMEM((pieces[k] * slot_n, n), BF16) for n in (2 * unit_n, feat_n)],
        )

    def join(first, width, *args):
        rows_n = 2 * token_n if width == half else token_n
        return call(functools.partial(join_kernel, first), [(rows_n, width)], *args)[0]

    own = pl.pallas_call(
        prepare_kernel,
        out_shape=jax.ShapeDtypeStruct((token_n, feat_n + TABLE), BF16),
        in_specs=[HBM] * 3,
        out_specs=VMEM,
        scratch_shapes=[
            pltpu.VMEM(routes.shape[::-1], jnp.int32),
            pltpu.VMEM(routes.shape[::-1], F32),
            pltpu.SemaphoreType.DMA((3,)),
        ],
        compiler_params=LIMIT,
    )(grad_out, routes.T, gate_weights.T)
    sibling = to_core(own)
    blocks = [[own, sibling]]
    moving = to_ring(jnp.concatenate(blocks[0], axis=0))
    acts = call(
        functools.partial(act_kernel, ring),
        [(p * slot_n, unit_n) for p in pieces],
        gate_act[0],
    )
    act_peer = to_side(acts[far])
    partials, mines, ups = [down(0)], {}, {}
    sents = [to_side(partials[0][1])]
    for k in range(1, far + 1):
        ended = [partials[k - 1][0]]
        if k < far:
            ended += [sents[k - 1]] + ([act_peer] if k == 1 else [])
        here = after(moving, *ended)
        if k < far - 1:
            moving = to_ring(here)
        elif k == far - 1:
            part = lax.dynamic_slice_in_dim(here, core * half, half, 1)
            moving = to_ring(jnp.concatenate([part, here[:, feat_n:]], axis=1))
        blocks.append([here, to_core(here, 64 if k == far else 128)])
        if k == far:
            mines[k - 1] = middle(k - 1, sents[k - 1])
            blocks[k][1] = after(blocks[k][1], mines[k - 1])
        partials.append(down(k))
        sents.append(to_side(partials[k][-2]))

    keep, give = up(far, partials[far][0], sents[far], acts[far], act_peer)
    peer = to_side(after(mines[far - 1], sents[far]))
    total = join(0, half, keep, *parts_to_core(give, 64))
    came = to_ring(total)
    came = [came[:token_n], came[token_n:]]
    peer = after(peer, total)
    for k in range(far - 1, 0, -1):
        keep, give = up(k, mines[k], peer)
        mines[k - 1] = middle(k - 1, after(sents[k - 1], peer))
        peer = to_side(mines[k - 1])
        rows = 128
        given = parts_to_core(give, rows)
        for i in range(2):
            parts = given[i * (token_n // rows) : (i + 1) * (token_n // rows)]
            total = join(i * token_n, feat_n, keep, *parts, came[i])
            came[i] = to_ring(total)
        came[0] = after(came[0], total)
        peer = after(peer, total)
    keep, give = up(0, mines[0], peer)
    total = to_core((came[0].astype(F32) + keep.astype(F32)).astype(BF16))
    return (came[1].astype(F32) + give.astype(F32) + total.astype(F32)).astype(BF16)


def spread_on_device(grad_out, routes, gate_weights, gate_act, w_down, w_up):
    experts_n = lax.axis_size("ep")
    slot_n = gate_act.shape[1] // experts_n
    rows_n = experts_n * slot_n
    token_n, choose_n = routes.shape
    flat_ids = routes.reshape(-1)
    one_hot = (flat_ids[:, None] == jnp.arange(experts_n, dtype=jnp.int32)[None, :]).astype(
        jnp.int32
    )
    earlier = jnp.cumsum(one_hot, axis=0) - one_hot
    slot_rank = jnp.sum(earlier * one_hot, axis=1)
    position = flat_ids * slot_n + slot_rank
    token_ids = jnp.arange(token_n * choose_n, dtype=jnp.int32) // choose_n
    token_of = jnp.full((rows_n,), token_n, jnp.int32).at[position].set(token_ids)
    weight_of = jnp.zeros((rows_n,), jnp.float32).at[position].set(gate_weights.reshape(-1))
    down_local = w_down[0]
    up_local = w_up[0]
    feat_part = grad_out.shape[1]
    padded = jnp.concatenate([grad_out, jnp.zeros((1, feat_part), grad_out.dtype)], axis=0)
    placed = (padded[token_of].astype(jnp.float32) * weight_of[:, None]).astype(jnp.bfloat16)
    placed = placed.reshape(experts_n, slot_n, feat_part)
    partial_value = jnp.einsum(
        "nsd,fd->nsf",
        lax.all_to_all(placed, "ep", split_axis=0, concat_axis=0, tiled=True),
        down_local,
        preferred_element_type=jnp.float32,
    )
    partial_value = partial_value.reshape(rows_n, -1)
    hidden_grad = lax.psum_scatter(
        partial_value.astype(jnp.bfloat16), "tp", scatter_dimension=1, tiled=True
    ).astype(jnp.float32)
    up_grad = (hidden_grad * gate_act[0].astype(jnp.float32)).astype(jnp.bfloat16)
    row_grad = lax.dot_general(
        lax.all_gather(up_grad, "tp", axis=1, tiled=True),
        up_local,
        (((1,), (1,)), ((), ())),
        preferred_element_type=jnp.float32,
    )
    row_grad = row_grad.astype(jnp.bfloat16).reshape(experts_n, slot_n, -1)
    returned = lax.all_to_all(row_grad, "ep", split_axis=0, concat_axis=0, tiled=True)
    picked = returned.reshape(rows_n, -1)[position]
    summed = jnp.sum(picked.astype(jnp.float32).reshape(token_n, choose_n, -1), axis=1)
    return summed.astype(jnp.bfloat16)


def solution(mesh):
    placed = (
        P("ep", "tp"),
        P("ep", None),
        P("ep", None),
        P("ep", None, "tp"),
        P("ep", None, "tp"),
        P("ep", "tp", None),
    )

    def whole(grad_out, routes, *rest):
        ep, tp = mesh.shape["ep"], mesh.shape["tp"]
        dense = tp == 2 and ep % 4 == 0 and 8 <= ep <= 2 * routes.shape[1]
        dense = dense and routes.shape[0] == 128 * ep and grad_out.shape[1] % 512 == 0
        return jax.shard_map(
            ring_on_device if dense else spread_on_device,
            mesh=mesh,
            in_specs=placed,
            out_specs=P("ep", "tp"),
            check_vma=False,
        )(grad_out, routes, *rest)

    return whole
```

```python
import functools

import jax
import jax.numpy as jnp
from jax import lax
from jax.experimental import pallas as pl
from jax.experimental.pallas import tpu as pltpu
from jax.sharding import PartitionSpec as P

BF16 = jnp.bfloat16
F32 = jnp.float32
VMEM = pl.BlockSpec(memory_space=pltpu.VMEM)
TABLE = 128
LIMIT = pltpu.CompilerParams(vmem_limit_bytes=16 * 1024 * 1024)


def dot_t(a, b):
    return lax.dot_general(a, b, (((1,), (1,)), ((), ())), preferred_element_type=F32)


def table_kernel(routes_ref, gates_ref, table_ref):
    choose_n, token_n = routes_ref.shape
    expert_n = lax.axis_size("ep")
    expert = lax.broadcasted_iota(jnp.int32, (expert_n, token_n), 0)
    chosen = jnp.zeros((expert_n, token_n), F32)
    weight = jnp.zeros((expert_n, token_n), F32)
    for k in range(choose_n):
        hit = routes_ref[k : k + 1, :] == expert
        chosen = jnp.where(hit, 1.0, chosen)
        weight = jnp.where(hit, gates_ref[k : k + 1, :], weight)
    first = lax.broadcasted_iota(jnp.int32, (token_n, token_n), 0)
    second = lax.broadcasted_iota(jnp.int32, (token_n, token_n), 1)
    earlier = jnp.where(first < second, 1.0, 0.0).astype(BF16)
    rank = jnp.dot(chosen.astype(BF16), earlier, preferred_element_type=F32)
    slot = jnp.where(chosen > 0.5, rank, -1.0)
    high = weight.astype(BF16).astype(F32)
    parts = [slot, high, weight - high]
    rest = jnp.zeros((TABLE - len(parts) * expert_n, token_n), F32)
    table_ref[...] = jnp.transpose(jnp.concatenate(parts + [rest], axis=0)).astype(BF16)


class Ring:
    def __init__(self, experts_n, slot_n, token_n):
        self.slot_n = slot_n
        self.token_n = token_n
        self.experts_n = experts_n
        self.chips_n = experts_n // 2
        self.far = self.chips_n // 2
        self.arrivals = [(0, 0), (0, 1)]
        for k in range(1, self.far):
            self.arrivals += [(k, 0), (k, 1), (-k, 1), (-k, 0)]
        self.arrivals += [(self.far, 0), (self.far, 1)]
        self.pieces = [2] + [4] * (self.far - 1) + [2]
        self.firsts = [sum(self.pieces[:k]) for k in range(self.far + 1)]

    def tables(self, chunk, refs):
        out = [(ref, at) for ref in refs for at in range(0, ref.shape[0], self.token_n)]
        return out[: self.pieces[chunk]]

    def chip(self, spot):
        return 2 * spot if spot < self.far else 2 * (self.chips_n - 1 - spot) + 1

    def pairs(self):
        out = []
        for i in range(self.experts_n):
            z, y = i // 4, i // 2 % 2
            spot = self.chips_n - 1 - z if y else z
            out.append((i, 2 * self.chip((spot + 1 - 2 * (i % 2)) % self.chips_n) + i % 2))
        return out

    def sources(self, chunk):
        me = lax.axis_index("ep")
        core = lax.rem(me, 2)
        z, y = me // 4, lax.rem(me // 2, 2)
        here = jnp.where(y == 1, self.chips_n - 1 - z, z)
        first = self.firsts[chunk]
        out = []
        for steps, flip in self.arrivals[first : first + self.pieces[chunk]]:
            spot = lax.rem(here + steps * (2 * core - 1) + self.chips_n, self.chips_n)
            chip = jnp.where(spot < self.far, 2 * spot, 2 * (self.chips_n - 1 - spot) + 1)
            out.append(2 * chip + (1 - core if flip else core))
        return out


def act_kernel(ring, act_ref, *out_refs):
    rows_n, slot_n = act_ref.shape[0], ring.slot_n
    for chunk, out_ref in enumerate(out_refs):
        part = out_ref.shape[0]
        row = lax.broadcasted_iota(jnp.int32, (part, 1), 0)
        target = row
        for b, source in enumerate(ring.sources(chunk)):
            target = jnp.where(row >= b * slot_n, row + (source - b) * slot_n, target)
        column = lax.broadcasted_iota(jnp.int32, (part, rows_n), 1)
        select = jnp.where(column == target, 1.0, 0.0).astype(BF16)
        out_ref[...] = jnp.dot(select, act_ref[...], preferred_element_type=F32).astype(BF16)


def mine_of(*columns):
    me, expert_n = lax.axis_index("ep"), lax.axis_size("ep")
    row = lax.broadcasted_iota(jnp.int32, (8, TABLE), 0)
    lane = lax.broadcasted_iota(jnp.int32, (8, TABLE), 1)
    hit = row < 0
    for i, parts in enumerate(columns):
        for part in parts:
            hit = hit | ((row == i) & (lane == part * expert_n + me))
    return jnp.where(hit, 1.0, 0.0).astype(BF16)


def down_kernel(ring, chunk, *refs):
    core, side = lax.rem(lax.axis_index("ep"), 2), lax.axis_index("tp")
    whole = chunk == ring.far
    outs_n = 1 if whole else 2
    blocks, w_ref = refs[: -3 - outs_n], refs[-3 - outs_n]
    outs, table_ref, rows_ref = refs[-2 - outs_n : -2], refs[-2], refs[-1]
    slot_n, token_n = ring.slot_n, ring.token_n
    feat_n = w_ref.shape[1]
    mine = mine_of((0,), (1, 2))
    slots, weights = [], []
    for b, (ref, at) in enumerate(ring.tables(chunk, blocks)):
        table = ref[at : at + token_n, ref.shape[1] - TABLE :]
        table_ref[b * token_n : (b + 1) * token_n, :] = table
        table = dot_t(mine, table)
        slots.append(jnp.where(table[0:1] >= 0.0, table[0:1] + float(b * slot_n), -1.0))
        weights.append(table[1:2])
    slots = jnp.concatenate(slots, axis=1).astype(jnp.int32)
    weights = jnp.concatenate(weights, axis=1)
    hit = lax.broadcasted_iota(jnp.int32, (rows_ref.shape[0], slots.shape[1]), 0) == slots
    weight = jnp.sum(jnp.where(hit, weights, 0.0), axis=1, keepdims=True)
    select = jnp.where(hit, 1.0, 0.0).astype(BF16)

    def chosen(select, parts):
        value, at = None, 0
        for ref in parts:
            rows = ref[:, : ref.shape[1] - TABLE]
            term = jnp.dot(select[:, at : at + ref.shape[0]], rows, preferred_element_type=F32)
            value = term if value is None else value + term
            at += ref.shape[0]
        return (value * weight).astype(BF16)

    if whole:
        half = feat_n // 2
        turned = jnp.concatenate([select[:, token_n:], select[:, :token_n]], axis=1)
        rows_ref[:, pl.ds(pl.multiple_of(core * half, 128), half)] = chosen(select, blocks[:1])
        rows_ref[:, pl.ds(pl.multiple_of((1 - core) * half, 128), half)] = chosen(turned, blocks[1:])
    else:
        rows_ref[...] = chosen(select, blocks)
    tile = 256
    if whole:
        (out_ref,) = outs
        for at in range(0, out_ref.shape[1], tile):
            out_ref[:, at : at + tile] = dot_t(rows_ref[...], w_ref[at : at + tile, :]).astype(BF16)
    else:
        unit = outs[0].shape[1]
        for out_ref, place in zip(outs, (side, 1 - side)):
            for t in range(0, unit, tile):
                at = pl.multiple_of(place * unit + t, tile)
                out_ref[:, t : t + tile] = dot_t(rows_ref[...], w_ref[pl.ds(at, tile), :]).astype(BF16)


def up_kernel(ring, chunk, table_ref, *refs):
    core, side = lax.rem(lax.axis_index("ep"), 2), lax.axis_index("tp")
    ins, (w_ref, keep_ref, give_ref, up_ref, row_ref) = refs[:-5], refs[-5:]
    slot_n, token_n = ring.slot_n, ring.token_n
    feat_n, unit = w_ref.shape[0], w_ref.shape[1] // 2
    mine_at = pl.multiple_of(side * unit, 128)
    peer_at = pl.multiple_of((1 - side) * unit, 128)
    if len(ins) == 2:
        up_ref[:, pl.ds(mine_at, unit)] = ins[0][...]
        up_ref[:, pl.ds(peer_at, unit)] = ins[1][...]
    else:
        for at, act_ref in ((mine_at, ins[2]), (peer_at, ins[3])):
            part = pl.ds(at, unit)
            hidden = ins[0][:, part].astype(F32) + ins[1][:, part].astype(F32)
            up_ref[:, part] = (hidden * act_ref[...].astype(F32)).astype(BF16)
    rows_n = up_ref.shape[0]
    tile = 256
    for t in range(0, feat_n, tile):
        row_ref[:, t : t + tile] = dot_t(up_ref[...], w_ref[t : t + tile, :]).astype(BF16)
    window = rows_n if rows_n <= 2 * slot_n else 2 * slot_n + (-2 * slot_n) % 16
    lane = lax.broadcasted_iota(jnp.int32, (token_n, window), 1)
    mine = mine_of((0,))
    selects, starts = [], []
    for b in range(ring.pieces[chunk]):
        start = 0 if b < 2 else rows_n - window
        table = table_ref[b * token_n : (b + 1) * token_n, :]
        slot = dot_t(table, mine)[:, 0:1].astype(jnp.int32)
        slot = jnp.where(slot >= 0, slot + (b * slot_n - start), -1)
        selects.append(jnp.where(lane == slot, 1.0, 0.0).astype(BF16))
        starts.append(start)

    def placed(b, sources_n, columns):
        select = jnp.concatenate(selects[b : b + sources_n], axis=0)
        rows = row_ref[starts[b] : starts[b] + window, columns]
        return jnp.dot(select, rows, preferred_element_type=F32).astype(BF16)

    if chunk == ring.far:
        half = feat_n // 2
        keep = placed(0, 2, pl.ds(pl.multiple_of(core * half, 128), half))
        keep_ref[:token_n, :] = keep[token_n:]
        keep_ref[token_n:, :] = keep[:token_n]
        give_ref[...] = placed(0, 2, pl.ds(pl.multiple_of((1 - core) * half, 128), half))
    else:
        sources_n = ring.pieces[chunk] // 2
        give_ref[...] = placed(0, sources_n, pl.ds(0, feat_n))
        keep_ref[...] = placed(sources_n, sources_n, pl.ds(0, feat_n))


def join_kernel(first, keep_ref, *refs):
    core = lax.rem(lax.axis_index("ep"), 2)
    out_ref = refs[-1]
    rows_n, feat_n = out_ref.shape
    given_refs, at = [], 0
    while at < rows_n:
        given_refs.append(refs[len(given_refs)])
        at += given_refs[-1].shape[0]
    came_refs = refs[len(given_refs) : -1]
    half = came_refs[0].shape[1] if came_refs else feat_n
    at = 0
    for given_ref in given_refs:
        rows = pl.ds(at, given_ref.shape[0])
        kept = pl.ds(first + at, given_ref.shape[0])

        def total(columns):
            return keep_ref[kept, columns].astype(F32) + given_ref[:, columns].astype(F32)

        if half == feat_n:
            value = total(pl.ds(0, feat_n))
            for came_ref in came_refs:
                value = value + came_ref[rows, :].astype(F32)
            out_ref[rows, :] = value.astype(BF16)
        else:
            mine = pl.ds(pl.multiple_of(core * half, 128), half)
            other = pl.ds(pl.multiple_of((1 - core) * half, 128), half)
            value = total(mine) + came_refs[0][rows, :].astype(F32)
            out_ref[rows, mine] = value.astype(BF16)
            out_ref[rows, other] = total(other).astype(BF16)
        at += given_ref.shape[0]


def after(value, *others):
    return lax.optimization_barrier((value, *others))[0]


def ring_on_device(grad_out, routes, gate_weights, gate_act, w_down, w_up):
    experts_n = lax.axis_size("ep")
    slot_n = gate_act.shape[1] // experts_n
    token_n = routes.shape[0]
    feat_n = grad_out.shape[1]
    half = feat_n // 2
    unit_n = gate_act.shape[2]
    ring = Ring(experts_n, slot_n, token_n)
    far, pieces = ring.far, ring.pieces
    split = 7 * token_n // 8
    streams = ((0, split), (split, 2 * token_n))
    swap = [(i, i ^ 1) for i in range(experts_n)]
    ring_pairs = ring.pairs()
    core = lax.axis_index("ep") % 2

    def parts_to_core(x, rows):
        return [lax.ppermute(p, "ep", swap) for p in jnp.split(x, x.shape[0] // rows)]

    def streams_to_core(x, *parts):
        return [
            [to_core(x[i:j], j - i) for i, j in zip(range(a, b, n), (*range(a + n, b, n), b))]
            for (a, b), n in zip(streams, parts)
        ]

    def to_core(x, rows=128):
        return jnp.concatenate(parts_to_core(x, rows), axis=0)

    def to_ring(x):
        return lax.ppermute(x, "ep", ring_pairs)

    def to_side(x):
        return lax.ppermute(x, "tp", [(0, 1), (1, 0)])

    def call(kernel, outs, *args, scratch=()):
        return pl.pallas_call(
            kernel,
            out_shape=[jax.ShapeDtypeStruct(shape, BF16) for shape in outs],
            in_specs=[VMEM] * len(args),
            out_specs=[VMEM] * len(outs),
            scratch_shapes=scratch,
            compiler_params=LIMIT,
        )(*args)

    def down(k):
        rows_n = pieces[k] * slot_n
        return call(
            functools.partial(down_kernel, ring, k),
            ([(rows_n, 2 * unit_n)] if k == far else [(rows_n, unit_n)] * 2)
            + [(pieces[k] * token_n, TABLE)],
            *blocks[k],
            w_down[0],
            scratch=[pltpu.VMEM((rows_n, feat_n), BF16)],
        )

    def middle(k, sent):
        hidden = partials[k][0].astype(F32) + sent.astype(F32)
        return (hidden * acts[k].astype(F32)).astype(BF16)

    def up(k, *args):
        shape = (2 * token_n, half) if k == far else (pieces[k] // 2 * token_n, feat_n)
        return call(
            functools.partial(up_kernel, ring, k),
            [shape] * 2,
            partials[k][-1],
            *args,
            w_up[0],
            scratch=[pltpu.VMEM((pieces[k] * slot_n, n), BF16) for n in (2 * unit_n, feat_n)],
        )

    def join(rows, width, *args):
        out = [(rows[1] - rows[0], width)]
        return call(functools.partial(join_kernel, rows[0]), out, *args)[0]

    sibling = to_core(grad_out)
    moving = to_ring(jnp.concatenate([grad_out, sibling], axis=0))
    (table,) = call(table_kernel, [(token_n, TABLE)], routes.T, gate_weights.T)
    tables = [table, to_core(table)]
    blocks = [[jnp.concatenate(x, axis=1) for x in zip([grad_out, sibling], tables)]]
    moving = jnp.concatenate([moving, to_ring(jnp.concatenate(tables, axis=0))], axis=1)
    acts = call(
        functools.partial(act_kernel, ring),
        [(p * slot_n, unit_n) for p in pieces],
        gate_act[0],
    )
    act_peer = to_side(acts[far])
    partials, mines, ups = [down(0)], {}, {}
    sents = [None]
    for k in range(1, far + 1):
        ended = [partials[k - 1][0]]
        if k < far:
            ended += [act_peer if k == 1 else sents[k - 1]]
        if k == far - 1:
            ended += [early]
        here = after(moving, *ended)
        if k < far - 1:
            moving = to_ring(here)
        elif k == far - 1:
            part = lax.dynamic_slice_in_dim(here, core * half, half, 1)
            moving = to_ring(jnp.concatenate([part, here[:, feat_n:]], axis=1))
        if k == far - 2:
            mines[k - 1] = middle(k - 1, sents[k - 1])
            early = to_side(mines[k - 1])
            here = after(here, mines[k - 1])
        blocks.append([here, to_core(here, 64 if k == far else 128)])
        if k == far:
            mines[k - 1] = middle(k - 1, sents[k - 1])
            blocks[k][1] = after(blocks[k][1], mines[k - 1])
        partials.append(down(k))
        sents.append(to_side(partials[k][-2]))

    ups[far - 3] = up(far - 3, mines[far - 3], after(early, partials[far][0]))
    swapped = streams_to_core(ups[far - 3][1], 64, 80)
    full = after(sents[far], ups[far - 3][0], *swapped[0], *swapped[1])
    keep, give = up(far, partials[far][0], full, acts[far], act_peer)
    peer = to_side(after(mines[far - 1], full))
    total = join((0, 2 * token_n), half, keep, *parts_to_core(give, 64))
    came = to_ring(total)
    came = [came[a:b] for a, b in streams]
    peer = after(peer, total)
    for k in range(far - 1, 0, -1):
        keep, give = ups[k] if k in ups else up(k, mines[k], peer)
        if k == far - 1:
            mines[k - 1] = middle(k - 1, after(sents[k - 1], peer))
            peer = to_side(mines[k - 1])
        elif k == far - 2:
            mines[0] = middle(0, to_side(after(partials[0][1], peer)))
            peer = to_side(mines[0])
        given = swapped if k in ups else streams_to_core(give, split if k == far - 1 else 64, 2 * token_n - split)
        totals = []
        for i in range(2):
            totals.append(join(streams[i], feat_n, keep, *given[i], came[i]))
            came[i] = to_ring(totals[i])
        came[0] = after(came[0], *totals)
        peer = after(peer, *totals)
    keep, give = up(0, mines[0], peer)
    total = [
        parts_to_core((x.astype(F32) + y.astype(F32)).astype(BF16), x.shape[0])[0]
        for x, y in ((came[0], keep[:split]), (came[1][: token_n - split], keep[split:]))
    ]
    total = jnp.concatenate(total, axis=0).astype(F32)
    return (came[1][token_n - split :].astype(F32) + give.astype(F32) + total).astype(BF16)


def spread_on_device(grad_out, routes, gate_weights, gate_act, w_down, w_up):
    experts_n = lax.axis_size("ep")
    slot_n = gate_act.shape[1] // experts_n
    rows_n = experts_n * slot_n
    token_n, choose_n = routes.shape
    flat_ids = routes.reshape(-1)
    one_hot = (flat_ids[:, None] == jnp.arange(experts_n, dtype=jnp.int32)[None, :]).astype(
        jnp.int32
    )
    earlier = jnp.cumsum(one_hot, axis=0) - one_hot
    slot_rank = jnp.sum(earlier * one_hot, axis=1)
    position = flat_ids * slot_n + slot_rank
    token_ids = jnp.arange(token_n * choose_n, dtype=jnp.int32) // choose_n
    token_of = jnp.full((rows_n,), token_n, jnp.int32).at[position].set(token_ids)
    weight_of = jnp.zeros((rows_n,), jnp.float32).at[position].set(gate_weights.reshape(-1))
    down_local = w_down[0]
    up_local = w_up[0]
    feat_part = grad_out.shape[1]
    padded = jnp.concatenate([grad_out, jnp.zeros((1, feat_part), grad_out.dtype)], axis=0)
    placed = (padded[token_of].astype(jnp.float32) * weight_of[:, None]).astype(jnp.bfloat16)
    placed = placed.reshape(experts_n, slot_n, feat_part)
    partial_value = jnp.einsum(
        "nsd,fd->nsf",
        lax.all_to_all(placed, "ep", split_axis=0, concat_axis=0, tiled=True),
        down_local,
        preferred_element_type=jnp.float32,
    )
    partial_value = partial_value.reshape(rows_n, -1)
    hidden_grad = lax.psum_scatter(
        partial_value.astype(jnp.bfloat16), "tp", scatter_dimension=1, tiled=True
    ).astype(jnp.float32)
    up_grad = (hidden_grad * gate_act[0].astype(jnp.float32)).astype(jnp.bfloat16)
    row_grad = lax.dot_general(
        lax.all_gather(up_grad, "tp", axis=1, tiled=True),
        up_local,
        (((1,), (1,)), ((), ())),
        preferred_element_type=jnp.float32,
    )
    row_grad = row_grad.astype(jnp.bfloat16).reshape(experts_n, slot_n, -1)
    returned = lax.all_to_all(row_grad, "ep", split_axis=0, concat_axis=0, tiled=True)
    picked = returned.reshape(rows_n, -1)[position]
    summed = jnp.sum(picked.astype(jnp.float32).reshape(token_n, choose_n, -1), axis=1)
    return summed.astype(jnp.bfloat16)


def solution(mesh):
    placed = (
        P("ep", "tp"),
        P("ep", None),
        P("ep", None),
        P("ep", None, "tp"),
        P("ep", None, "tp"),
        P("ep", "tp", None),
    )

    def whole(grad_out, routes, *rest):
        ep, tp = mesh.shape["ep"], mesh.shape["tp"]
        dense = tp == 2 and ep % 4 == 0 and 8 <= ep <= 2 * routes.shape[1]
        dense = dense and routes.shape[0] == 128 * ep and grad_out.shape[1] % 512 == 0
        return jax.shard_map(
            ring_on_device if dense else spread_on_device,
            mesh=mesh,
            in_specs=placed,
            out_specs=P("ep", "tp"),
            check_vma=False,
        )(grad_out, routes, *rest)

    return whole
```

```python
import functools

import jax
import jax.numpy as jnp
from jax import lax
from jax.experimental import pallas as pl
from jax.experimental.pallas import tpu as pltpu
from jax.sharding import PartitionSpec as P

BF16 = jnp.bfloat16
F32 = jnp.float32
VMEM = pl.BlockSpec(memory_space=pltpu.VMEM)
TABLE = 128
LIMIT = pltpu.CompilerParams(vmem_limit_bytes=16 * 1024 * 1024)


def dot_t(a, b):
    return lax.dot_general(a, b, (((1,), (1,)), ((), ())), preferred_element_type=F32)


def table_kernel(routes_ref, gates_ref, table_ref):
    choose_n, token_n = routes_ref.shape
    expert_n = lax.axis_size("ep")
    expert = lax.broadcasted_iota(jnp.int32, (expert_n, token_n), 0)
    chosen = jnp.zeros((expert_n, token_n), F32)
    weight = jnp.zeros((expert_n, token_n), F32)
    for k in range(choose_n):
        hit = routes_ref[k : k + 1, :] == expert
        chosen = jnp.where(hit, 1.0, chosen)
        weight = jnp.where(hit, gates_ref[k : k + 1, :], weight)
    first = lax.broadcasted_iota(jnp.int32, (token_n, token_n), 0)
    second = lax.broadcasted_iota(jnp.int32, (token_n, token_n), 1)
    earlier = jnp.where(first < second, 1.0, 0.0).astype(BF16)
    rank = jnp.dot(chosen.astype(BF16), earlier, preferred_element_type=F32)
    slot = jnp.where(chosen > 0.5, rank, -1.0)
    high = weight.astype(BF16).astype(F32)
    parts = [slot, high, weight - high]
    rest = jnp.zeros((TABLE - len(parts) * expert_n, token_n), F32)
    table_ref[...] = jnp.transpose(jnp.concatenate(parts + [rest], axis=0)).astype(BF16)


class Ring:
    def __init__(self, experts_n, slot_n, token_n):
        self.slot_n = slot_n
        self.token_n = token_n
        self.experts_n = experts_n
        self.chips_n = experts_n // 2
        self.far = self.chips_n // 2
        self.arrivals = [(0, 0), (0, 1)]
        for k in range(1, self.far):
            self.arrivals += [(k, 0), (k, 1), (-k, 1), (-k, 0)]
        self.arrivals += [(self.far, 0), (self.far, 1)]
        self.pieces = [2] + [4] * (self.far - 1) + [2]
        self.firsts = [sum(self.pieces[:k]) for k in range(self.far + 1)]

    def tables(self, chunk, refs):
        out = [(ref, at) for ref in refs for at in range(0, ref.shape[0], self.token_n)]
        return out[: self.pieces[chunk]]

    def chip(self, spot):
        return 2 * spot if spot < self.far else 2 * (self.chips_n - 1 - spot) + 1

    def pairs(self):
        out = []
        for i in range(self.experts_n):
            z, y = i // 4, i // 2 % 2
            spot = self.chips_n - 1 - z if y else z
            out.append((i, 2 * self.chip((spot + 1 - 2 * (i % 2)) % self.chips_n) + i % 2))
        return out

    def sources(self, chunk):
        me = lax.axis_index("ep")
        core = lax.rem(me, 2)
        z, y = me // 4, lax.rem(me // 2, 2)
        here = jnp.where(y == 1, self.chips_n - 1 - z, z)
        first = self.firsts[chunk]
        out = []
        for steps, flip in self.arrivals[first : first + self.pieces[chunk]]:
            spot = lax.rem(here + steps * (2 * core - 1) + self.chips_n, self.chips_n)
            chip = jnp.where(spot < self.far, 2 * spot, 2 * (self.chips_n - 1 - spot) + 1)
            out.append(2 * chip + (1 - core if flip else core))
        return out


def act_kernel(ring, act_ref, *out_refs):
    rows_n, slot_n = act_ref.shape[0], ring.slot_n
    for chunk, out_ref in enumerate(out_refs):
        part = out_ref.shape[0]
        row = lax.broadcasted_iota(jnp.int32, (part, 1), 0)
        target = row
        for b, source in enumerate(ring.sources(chunk)):
            target = jnp.where(row >= b * slot_n, row + (source - b) * slot_n, target)
        column = lax.broadcasted_iota(jnp.int32, (part, rows_n), 1)
        select = jnp.where(column == target, 1.0, 0.0).astype(BF16)
        out_ref[...] = jnp.dot(select, act_ref[...], preferred_element_type=F32).astype(BF16)


def mine_of(*columns):
    me, expert_n = lax.axis_index("ep"), lax.axis_size("ep")
    row = lax.broadcasted_iota(jnp.int32, (8, TABLE), 0)
    lane = lax.broadcasted_iota(jnp.int32, (8, TABLE), 1)
    hit = row < 0
    for i, parts in enumerate(columns):
        for part in parts:
            hit = hit | ((row == i) & (lane == part * expert_n + me))
    return jnp.where(hit, 1.0, 0.0).astype(BF16)


def down_kernel(ring, chunk, *refs):
    core, side = lax.rem(lax.axis_index("ep"), 2), lax.axis_index("tp")
    whole = chunk == ring.far
    outs_n = 1 if whole else 2
    blocks, w_ref = refs[: -3 - outs_n], refs[-3 - outs_n]
    outs, table_ref, rows_ref = refs[-2 - outs_n : -2], refs[-2], refs[-1]
    slot_n, token_n = ring.slot_n, ring.token_n
    feat_n = w_ref.shape[1]
    mine = mine_of((0,), (1, 2))
    slots, weights = [], []
    for b, (ref, at) in enumerate(ring.tables(chunk, blocks)):
        table = ref[at : at + token_n, ref.shape[1] - TABLE :]
        table_ref[b * token_n : (b + 1) * token_n, :] = table
        table = dot_t(mine, table)
        slots.append(jnp.where(table[0:1] >= 0.0, table[0:1] + float(b * slot_n), -1.0))
        weights.append(table[1:2])
    slots = jnp.concatenate(slots, axis=1).astype(jnp.int32)
    weights = jnp.concatenate(weights, axis=1)
    hit = lax.broadcasted_iota(jnp.int32, (rows_ref.shape[0], slots.shape[1]), 0) == slots
    weight = jnp.sum(jnp.where(hit, weights, 0.0), axis=1, keepdims=True)
    select = jnp.where(hit, 1.0, 0.0).astype(BF16)

    def chosen(select, parts):
        value, at = None, 0
        for ref in parts:
            rows = ref[:, : ref.shape[1] - TABLE]
            term = jnp.dot(select[:, at : at + ref.shape[0]], rows, preferred_element_type=F32)
            value = term if value is None else value + term
            at += ref.shape[0]
        return (value * weight).astype(BF16)

    if whole:
        half = feat_n // 2
        turned = jnp.concatenate([select[:, token_n:], select[:, :token_n]], axis=1)
        rows_ref[:, pl.ds(pl.multiple_of(core * half, 128), half)] = chosen(select, blocks[:1])
        rows_ref[:, pl.ds(pl.multiple_of((1 - core) * half, 128), half)] = chosen(turned, blocks[1:])
    else:
        rows_ref[...] = chosen(select, blocks)
    tile = 256
    if whole:
        (out_ref,) = outs
        for at in range(0, out_ref.shape[1], tile):
            out_ref[:, at : at + tile] = dot_t(rows_ref[...], w_ref[at : at + tile, :]).astype(BF16)
    else:
        unit = outs[0].shape[1]
        for out_ref, place in zip(outs, (side, 1 - side)):
            for t in range(0, unit, tile):
                at = pl.multiple_of(place * unit + t, tile)
                out_ref[:, t : t + tile] = dot_t(rows_ref[...], w_ref[pl.ds(at, tile), :]).astype(BF16)


def up_kernel(ring, chunk, table_ref, *refs):
    core, side = lax.rem(lax.axis_index("ep"), 2), lax.axis_index("tp")
    ins, (w_ref, keep_ref, give_ref, up_ref, row_ref) = refs[:-5], refs[-5:]
    slot_n, token_n = ring.slot_n, ring.token_n
    feat_n, unit = w_ref.shape[0], w_ref.shape[1] // 2
    mine_at = pl.multiple_of(side * unit, 128)
    peer_at = pl.multiple_of((1 - side) * unit, 128)
    if len(ins) == 2:
        up_ref[:, pl.ds(mine_at, unit)] = ins[0][...]
        up_ref[:, pl.ds(peer_at, unit)] = ins[1][...]
    else:
        for at, act_ref in ((mine_at, ins[2]), (peer_at, ins[3])):
            part = pl.ds(at, unit)
            hidden = ins[0][:, part].astype(F32) + ins[1][:, part].astype(F32)
            up_ref[:, part] = (hidden * act_ref[...].astype(F32)).astype(BF16)
    rows_n = up_ref.shape[0]
    tile = 256
    for t in range(0, feat_n, tile):
        row_ref[:, t : t + tile] = dot_t(up_ref[...], w_ref[t : t + tile, :]).astype(BF16)
    window = rows_n if rows_n <= 2 * slot_n else 2 * slot_n + (-2 * slot_n) % 16
    lane = lax.broadcasted_iota(jnp.int32, (token_n, window), 1)
    mine = mine_of((0,))
    selects, starts = [], []
    for b in range(ring.pieces[chunk]):
        start = 0 if b < 2 else rows_n - window
        table = table_ref[b * token_n : (b + 1) * token_n, :]
        slot = dot_t(table, mine)[:, 0:1].astype(jnp.int32)
        slot = jnp.where(slot >= 0, slot + (b * slot_n - start), -1)
        selects.append(jnp.where(lane == slot, 1.0, 0.0).astype(BF16))
        starts.append(start)

    def placed(b, sources_n, columns):
        select = jnp.concatenate(selects[b : b + sources_n], axis=0)
        rows = row_ref[starts[b] : starts[b] + window, columns]
        return jnp.dot(select, rows, preferred_element_type=F32).astype(BF16)

    if chunk == ring.far:
        half = feat_n // 2
        keep = placed(0, 2, pl.ds(pl.multiple_of(core * half, 128), half))
        keep_ref[:token_n, :] = keep[token_n:]
        keep_ref[token_n:, :] = keep[:token_n]
        give_ref[...] = placed(0, 2, pl.ds(pl.multiple_of((1 - core) * half, 128), half))
    else:
        sources_n = ring.pieces[chunk] // 2
        give_ref[...] = placed(0, sources_n, pl.ds(0, feat_n))
        keep_ref[...] = placed(sources_n, sources_n, pl.ds(0, feat_n))


def join_kernel(first, keep_ref, *refs):
    core = lax.rem(lax.axis_index("ep"), 2)
    out_ref = refs[-1]
    rows_n, feat_n = out_ref.shape
    given_refs, at = [], 0
    while at < rows_n:
        given_refs.append(refs[len(given_refs)])
        at += given_refs[-1].shape[0]
    came_refs = refs[len(given_refs) : -1]
    half = came_refs[0].shape[1] if came_refs else feat_n
    at = 0
    for given_ref in given_refs:
        rows = pl.ds(at, given_ref.shape[0])
        kept = pl.ds(first + at, given_ref.shape[0])

        def total(columns):
            return keep_ref[kept, columns].astype(F32) + given_ref[:, columns].astype(F32)

        if half == feat_n:
            value = total(pl.ds(0, feat_n))
            for came_ref in came_refs:
                value = value + came_ref[rows, :].astype(F32)
            out_ref[rows, :] = value.astype(BF16)
        else:
            mine = pl.ds(pl.multiple_of(core * half, 128), half)
            other = pl.ds(pl.multiple_of((1 - core) * half, 128), half)
            value = total(mine) + came_refs[0][rows, :].astype(F32)
            out_ref[rows, mine] = value.astype(BF16)
            out_ref[rows, other] = total(other).astype(BF16)
        at += given_ref.shape[0]


def after(value, *others):
    return lax.optimization_barrier((value, *others))[0]


def ring_on_device(grad_out, routes, gate_weights, gate_act, w_down, w_up):
    experts_n = lax.axis_size("ep")
    slot_n = gate_act.shape[1] // experts_n
    token_n = routes.shape[0]
    feat_n = grad_out.shape[1]
    half = feat_n // 2
    unit_n = gate_act.shape[2]
    ring = Ring(experts_n, slot_n, token_n)
    far, pieces = ring.far, ring.pieces
    split = 7 * token_n // 8
    streams = ((0, split), (split, 2 * token_n))
    swap = [(i, i ^ 1) for i in range(experts_n)]
    ring_pairs = ring.pairs()
    core = lax.axis_index("ep") % 2

    def parts_to_core(x, rows):
        return [lax.ppermute(p, "ep", swap) for p in jnp.split(x, x.shape[0] // rows)]

    def streams_to_core(x, *parts):
        return [
            [to_core(x[i:j], j - i) for i, j in zip(range(a, b, n), (*range(a + n, b, n), b))]
            for (a, b), n in zip(streams, parts)
        ]

    def to_core(x, rows=128):
        return jnp.concatenate(parts_to_core(x, rows), axis=0)

    def to_ring(x):
        return lax.ppermute(x, "ep", ring_pairs)

    def to_side(x):
        return lax.ppermute(x, "tp", [(0, 1), (1, 0)])

    def call(kernel, outs, *args, scratch=()):
        return pl.pallas_call(
            kernel,
            out_shape=[jax.ShapeDtypeStruct(shape, BF16) for shape in outs],
            in_specs=[VMEM] * len(args),
            out_specs=[VMEM] * len(outs),
            scratch_shapes=scratch,
            compiler_params=LIMIT,
        )(*args)

    def down(k):
        rows_n = pieces[k] * slot_n
        return call(
            functools.partial(down_kernel, ring, k),
            ([(rows_n, 2 * unit_n)] if k == far else [(rows_n, unit_n)] * 2)
            + [(pieces[k] * token_n, TABLE)],
            *blocks[k],
            w_down[0],
            scratch=[pltpu.VMEM((rows_n, feat_n), BF16)],
        )

    def middle(k, sent):
        hidden = partials[k][0].astype(F32) + sent.astype(F32)
        return (hidden * acts[k].astype(F32)).astype(BF16)

    def up(k, *args):
        shape = (2 * token_n, half) if k == far else (pieces[k] // 2 * token_n, feat_n)
        return call(
            functools.partial(up_kernel, ring, k),
            [shape] * 2,
            partials[k][-1],
            *args,
            w_up[0],
            scratch=[pltpu.VMEM((pieces[k] * slot_n, n), BF16) for n in (2 * unit_n, feat_n)],
        )

    def join(rows, width, *args):
        out = [(rows[1] - rows[0], width)]
        return call(functools.partial(join_kernel, rows[0]), out, *args)[0]

    sibling = to_core(grad_out)
    moving = jnp.concatenate([to_ring(grad_out), to_ring(sibling)], axis=0)
    (table,) = call(table_kernel, [(token_n, TABLE)], routes.T, gate_weights.T)
    tables = [table, to_core(table)]
    blocks = [[jnp.concatenate(x, axis=1) for x in zip([grad_out, sibling], tables)]]
    moving = jnp.concatenate([moving, to_ring(jnp.concatenate(tables, axis=0))], axis=1)
    acts = call(
        functools.partial(act_kernel, ring),
        [(p * slot_n, unit_n) for p in pieces],
        gate_act[0],
    )
    act_peer = to_side(acts[far])
    partials, mines, ups = [down(0)], {}, {}
    sents = [None]
    for k in range(1, far + 1):
        ended = [partials[k - 1][0]] if k > 1 else []
        if k == 2:
            ended += [partials[0][0], act_peer]
        if k < far:
            ended += [acts[0] if k == 1 else sents[k - 1]]
        if k == far - 1:
            ended += [early]
        here = after(moving, *ended)
        if k < far - 1:
            moving = to_ring(here)
        elif k == far - 1:
            part = lax.dynamic_slice_in_dim(here, core * half, half, 1)
            moving = to_ring(jnp.concatenate([part, here[:, feat_n:]], axis=1))
        if k == far - 2:
            mines[k - 1] = middle(k - 1, sents[k - 1])
            early = to_side(mines[k - 1])
            here = after(here, mines[k - 1])
        blocks.append([here, to_core(here, 64 if k == far else 128)])
        if k == far:
            mines[k - 1] = middle(k - 1, sents[k - 1])
            blocks[k][1] = after(blocks[k][1], mines[k - 1])
        partials.append(down(k))
        sents.append(to_side(partials[k][-2]))

    ups[far - 3] = up(far - 3, mines[far - 3], after(early, partials[far][0]))
    swapped = streams_to_core(ups[far - 3][1], 64, 80)
    full = after(sents[far], ups[far - 3][0], *swapped[0], *swapped[1])
    keep, give = up(far, partials[far][0], full, acts[far], act_peer)
    peer = to_side(after(mines[far - 1], full))
    total = join((0, 2 * token_n), half, keep, *parts_to_core(give, 128))
    came = to_ring(total)
    came = [came[a:b] for a, b in streams]
    peer = after(peer, total)
    for k in range(far - 1, 0, -1):
        if k == far - 1:
            mines[k - 1] = middle(k - 1, after(sents[k - 1], peer))
            mines[k] = after(mines[k], mines[k - 1])
        keep, give = ups[k] if k in ups else up(k, mines[k], peer)
        if k == far - 1:
            peer = to_side(mines[k - 1])
        elif k == far - 2:
            mines[0] = middle(0, to_side(after(partials[0][1], peer)))
            peer = to_side(mines[0])
        given = swapped if k in ups else streams_to_core(give, split if k == far - 1 else 64, 2 * token_n - split)
        totals = []
        for i in range(2):
            totals.append(join(streams[i], feat_n, keep, *given[i], came[i]))
            came[i] = to_ring(totals[i])
        came[0] = after(came[0], *totals)
        peer = after(peer, *totals)
    keep, give = up(0, mines[0], peer)
    total = [
        parts_to_core((x.astype(F32) + y.astype(F32)).astype(BF16), x.shape[0])[0]
        for x, y in ((came[0], keep[:split]), (came[1][: token_n - split], keep[split:]))
    ]
    total = jnp.concatenate(total, axis=0).astype(F32)
    return (came[1][token_n - split :].astype(F32) + give.astype(F32) + total).astype(BF16)


def spread_on_device(grad_out, routes, gate_weights, gate_act, w_down, w_up):
    experts_n = lax.axis_size("ep")
    slot_n = gate_act.shape[1] // experts_n
    rows_n = experts_n * slot_n
    token_n, choose_n = routes.shape
    flat_ids = routes.reshape(-1)
    one_hot = (flat_ids[:, None] == jnp.arange(experts_n, dtype=jnp.int32)[None, :]).astype(
        jnp.int32
    )
    earlier = jnp.cumsum(one_hot, axis=0) - one_hot
    slot_rank = jnp.sum(earlier * one_hot, axis=1)
    position = flat_ids * slot_n + slot_rank
    token_ids = jnp.arange(token_n * choose_n, dtype=jnp.int32) // choose_n
    token_of = jnp.full((rows_n,), token_n, jnp.int32).at[position].set(token_ids)
    weight_of = jnp.zeros((rows_n,), jnp.float32).at[position].set(gate_weights.reshape(-1))
    down_local = w_down[0]
    up_local = w_up[0]
    feat_part = grad_out.shape[1]
    padded = jnp.concatenate([grad_out, jnp.zeros((1, feat_part), grad_out.dtype)], axis=0)
    placed = (padded[token_of].astype(jnp.float32) * weight_of[:, None]).astype(jnp.bfloat16)
    placed = placed.reshape(experts_n, slot_n, feat_part)
    partial_value = jnp.einsum(
        "nsd,fd->nsf",
        lax.all_to_all(placed, "ep", split_axis=0, concat_axis=0, tiled=True),
        down_local,
        preferred_element_type=jnp.float32,
    )
    partial_value = partial_value.reshape(rows_n, -1)
    hidden_grad = lax.psum_scatter(
        partial_value.astype(jnp.bfloat16), "tp", scatter_dimension=1, tiled=True
    ).astype(jnp.float32)
    up_grad = (hidden_grad * gate_act[0].astype(jnp.float32)).astype(jnp.bfloat16)
    row_grad = lax.dot_general(
        lax.all_gather(up_grad, "tp", axis=1, tiled=True),
        up_local,
        (((1,), (1,)), ((), ())),
        preferred_element_type=jnp.float32,
    )
    row_grad = row_grad.astype(jnp.bfloat16).reshape(experts_n, slot_n, -1)
    returned = lax.all_to_all(row_grad, "ep", split_axis=0, concat_axis=0, tiled=True)
    picked = returned.reshape(rows_n, -1)[position]
    summed = jnp.sum(picked.astype(jnp.float32).reshape(token_n, choose_n, -1), axis=1)
    return summed.astype(jnp.bfloat16)


def solution(mesh):
    placed = (
        P("ep", "tp"),
        P("ep", None),
        P("ep", None),
        P("ep", None, "tp"),
        P("ep", None, "tp"),
        P("ep", "tp", None),
    )

    def whole(grad_out, routes, *rest):
        ep, tp = mesh.shape["ep"], mesh.shape["tp"]
        dense = tp == 2 and ep % 4 == 0 and 8 <= ep <= 2 * routes.shape[1]
        dense = dense and routes.shape[0] == 128 * ep and grad_out.shape[1] % 512 == 0
        return jax.shard_map(
            ring_on_device if dense else spread_on_device,
            mesh=mesh,
            in_specs=placed,
            out_specs=P("ep", "tp"),
            check_vma=False,
        )(grad_out, routes, *rest)

    return whole
```

```python
import functools

import jax
import jax.numpy as jnp
from jax import lax
from jax.experimental import pallas as pl
from jax.experimental.pallas import tpu as pltpu
from jax.sharding import PartitionSpec as P

BF16 = jnp.bfloat16
F32 = jnp.float32
VMEM = pl.BlockSpec(memory_space=pltpu.VMEM)
TABLE = 128
LIMIT = pltpu.CompilerParams(vmem_limit_bytes=16 * 1024 * 1024)


def dot_t(a, b):
    return lax.dot_general(a, b, (((1,), (1,)), ((), ())), preferred_element_type=F32)


def table_kernel(routes_ref, gates_ref, table_ref):
    choose_n, token_n = routes_ref.shape
    expert_n = lax.axis_size("ep")
    expert = lax.broadcasted_iota(jnp.int32, (expert_n, token_n), 0)
    chosen = jnp.zeros((expert_n, token_n), F32)
    weight = jnp.zeros((expert_n, token_n), F32)
    for k in range(choose_n):
        hit = routes_ref[k : k + 1, :] == expert
        chosen = jnp.where(hit, 1.0, chosen)
        weight = jnp.where(hit, gates_ref[k : k + 1, :], weight)
    first = lax.broadcasted_iota(jnp.int32, (token_n, token_n), 0)
    second = lax.broadcasted_iota(jnp.int32, (token_n, token_n), 1)
    earlier = jnp.where(first < second, 1.0, 0.0).astype(BF16)
    rank = jnp.dot(chosen.astype(BF16), earlier, preferred_element_type=F32)
    slot = jnp.where(chosen > 0.5, rank, -1.0)
    high = weight.astype(BF16).astype(F32)
    parts = [slot, high, weight - high]
    rest = jnp.zeros((TABLE - len(parts) * expert_n, token_n), F32)
    table_ref[...] = jnp.transpose(jnp.concatenate(parts + [rest], axis=0)).astype(BF16)


class Ring:
    def __init__(self, experts_n, slot_n, token_n):
        self.slot_n = slot_n
        self.token_n = token_n
        self.experts_n = experts_n
        self.chips_n = experts_n // 2
        self.far = self.chips_n // 2
        self.arrivals = [(0, 0), (0, 1)]
        for k in range(1, self.far):
            self.arrivals += [(k, 0), (k, 1), (-k, 1), (-k, 0)]
        self.arrivals += [(self.far, 0), (self.far, 1)]
        self.pieces = [2] + [4] * (self.far - 1) + [2]
        self.firsts = [sum(self.pieces[:k]) for k in range(self.far + 1)]

    def tables(self, chunk, refs):
        out = [(ref, at) for ref in refs for at in range(0, ref.shape[0], self.token_n)]
        return out[: self.pieces[chunk]]

    def chip(self, spot):
        return 2 * spot if spot < self.far else 2 * (self.chips_n - 1 - spot) + 1

    def pairs(self):
        out = []
        for i in range(self.experts_n):
            z, y = i // 4, i // 2 % 2
            spot = self.chips_n - 1 - z if y else z
            out.append((i, 2 * self.chip((spot + 1 - 2 * (i % 2)) % self.chips_n) + i % 2))
        return out

    def sources(self, chunk):
        me = lax.axis_index("ep")
        core = lax.rem(me, 2)
        z, y = me // 4, lax.rem(me // 2, 2)
        here = jnp.where(y == 1, self.chips_n - 1 - z, z)
        first = self.firsts[chunk]
        out = []
        for steps, flip in self.arrivals[first : first + self.pieces[chunk]]:
            spot = lax.rem(here + steps * (2 * core - 1) + self.chips_n, self.chips_n)
            chip = jnp.where(spot < self.far, 2 * spot, 2 * (self.chips_n - 1 - spot) + 1)
            out.append(2 * chip + (1 - core if flip else core))
        return out


def act_kernel(ring, act_ref, *out_refs):
    rows_n, slot_n = act_ref.shape[0], ring.slot_n
    for chunk, out_ref in enumerate(out_refs):
        part = out_ref.shape[0]
        row = lax.broadcasted_iota(jnp.int32, (part, 1), 0)
        target = row
        for b, source in enumerate(ring.sources(chunk)):
            target = jnp.where(row >= b * slot_n, row + (source - b) * slot_n, target)
        column = lax.broadcasted_iota(jnp.int32, (part, rows_n), 1)
        select = jnp.where(column == target, 1.0, 0.0).astype(BF16)
        out_ref[...] = jnp.dot(select, act_ref[...], preferred_element_type=F32).astype(BF16)


def mine_of(*columns):
    me, expert_n = lax.axis_index("ep"), lax.axis_size("ep")
    row = lax.broadcasted_iota(jnp.int32, (8, TABLE), 0)
    lane = lax.broadcasted_iota(jnp.int32, (8, TABLE), 1)
    hit = row < 0
    for i, parts in enumerate(columns):
        for part in parts:
            hit = hit | ((row == i) & (lane == part * expert_n + me))
    return jnp.where(hit, 1.0, 0.0).astype(BF16)


def down_kernel(ring, chunk, *refs):
    core, side = lax.rem(lax.axis_index("ep"), 2), lax.axis_index("tp")
    whole = chunk == ring.far
    outs_n = 1 if whole else 2
    blocks, w_ref = refs[: -3 - outs_n], refs[-3 - outs_n]
    outs, table_ref, rows_ref = refs[-2 - outs_n : -2], refs[-2], refs[-1]
    slot_n, token_n = ring.slot_n, ring.token_n
    feat_n = w_ref.shape[1]
    mine = mine_of((0,), (1, 2))
    slots, weights = [], []
    for b, (ref, at) in enumerate(ring.tables(chunk, blocks)):
        table = ref[at : at + token_n, ref.shape[1] - TABLE :]
        table_ref[b * token_n : (b + 1) * token_n, :] = table
        table = dot_t(mine, table)
        slots.append(jnp.where(table[0:1] >= 0.0, table[0:1] + float(b * slot_n), -1.0))
        weights.append(table[1:2])
    slots = jnp.concatenate(slots, axis=1).astype(jnp.int32)
    weights = jnp.concatenate(weights, axis=1)
    hit = lax.broadcasted_iota(jnp.int32, (rows_ref.shape[0], slots.shape[1]), 0) == slots
    weight = jnp.sum(jnp.where(hit, weights, 0.0), axis=1, keepdims=True)
    select = jnp.where(hit, 1.0, 0.0).astype(BF16)

    def chosen(select, parts):
        value, at = None, 0
        for ref in parts:
            rows = ref[:, : ref.shape[1] - TABLE]
            term = jnp.dot(select[:, at : at + ref.shape[0]], rows, preferred_element_type=F32)
            value = term if value is None else value + term
            at += ref.shape[0]
        return (value * weight).astype(BF16)

    if whole:
        half = feat_n // 2
        turned = jnp.concatenate([select[:, token_n:], select[:, :token_n]], axis=1)
        rows_ref[:, pl.ds(pl.multiple_of(core * half, 128), half)] = chosen(select, blocks[:1])
        rows_ref[:, pl.ds(pl.multiple_of((1 - core) * half, 128), half)] = chosen(turned, blocks[1:])
    else:
        rows_ref[...] = chosen(select, blocks)
    tile = 256
    if whole:
        (out_ref,) = outs
        for at in range(0, out_ref.shape[1], tile):
            out_ref[:, at : at + tile] = dot_t(rows_ref[...], w_ref[at : at + tile, :]).astype(BF16)
    else:
        unit = outs[0].shape[1]
        for out_ref, place in zip(outs, (side, 1 - side)):
            for t in range(0, unit, tile):
                at = pl.multiple_of(place * unit + t, tile)
                out_ref[:, t : t + tile] = dot_t(rows_ref[...], w_ref[pl.ds(at, tile), :]).astype(BF16)


def up_kernel(ring, chunk, table_ref, *refs):
    core, side = lax.rem(lax.axis_index("ep"), 2), lax.axis_index("tp")
    ins, (w_ref, keep_ref, give_ref, up_ref, row_ref) = refs[:-5], refs[-5:]
    slot_n, token_n = ring.slot_n, ring.token_n
    feat_n, unit = w_ref.shape[0], w_ref.shape[1] // 2
    mine_at = pl.multiple_of(side * unit, 128)
    peer_at = pl.multiple_of((1 - side) * unit, 128)
    if len(ins) == 2:
        up_ref[:, pl.ds(mine_at, unit)] = ins[0][...]
        up_ref[:, pl.ds(peer_at, unit)] = ins[1][...]
    else:
        for at, act_ref in ((mine_at, ins[2]), (peer_at, ins[3])):
            part = pl.ds(at, unit)
            hidden = ins[0][:, part].astype(F32) + ins[1][:, part].astype(F32)
            up_ref[:, part] = (hidden * act_ref[...].astype(F32)).astype(BF16)
    rows_n = up_ref.shape[0]
    tile = 256
    for t in range(0, feat_n, tile):
        row_ref[:, t : t + tile] = dot_t(up_ref[...], w_ref[t : t + tile, :]).astype(BF16)
    if rows_n <= 2 * slot_n:
        windows = [(0, rows_n)]
    else:
        windows = [(0, 2 * slot_n + (-2 * slot_n) % 16), (2 * slot_n // 16 * 16, rows_n)]
    mine = mine_of((0,))
    selects = []
    for b in range(ring.pieces[chunk]):
        start, end = windows[b // 2]
        lane = lax.broadcasted_iota(jnp.int32, (token_n, end - start), 1)
        table = table_ref[b * token_n : (b + 1) * token_n, :]
        slot = dot_t(table, mine)[:, 0:1].astype(jnp.int32)
        slot = jnp.where(slot >= 0, slot + (b * slot_n - start), -1)
        selects.append(jnp.where(lane == slot, 1.0, 0.0).astype(BF16))

    def placed(b, sources_n, columns):
        select = jnp.concatenate(selects[b : b + sources_n], axis=0)
        start, end = windows[b // 2]
        rows = row_ref[start:end, columns]
        return jnp.dot(select, rows, preferred_element_type=F32).astype(BF16)

    if chunk == ring.far:
        half = feat_n // 2
        keep = placed(0, 2, pl.ds(pl.multiple_of(core * half, 128), half))
        keep_ref[:token_n, :] = keep[token_n:]
        keep_ref[token_n:, :] = keep[:token_n]
        give_ref[...] = placed(0, 2, pl.ds(pl.multiple_of((1 - core) * half, 128), half))
    else:
        sources_n = ring.pieces[chunk] // 2
        give_ref[...] = placed(0, sources_n, pl.ds(0, feat_n))
        keep_ref[...] = placed(sources_n, sources_n, pl.ds(0, feat_n))


def join_kernel(first, keep_ref, *refs):
    core = lax.rem(lax.axis_index("ep"), 2)
    out_ref = refs[-1]
    rows_n, feat_n = out_ref.shape
    given_refs, at = [], 0
    while at < rows_n:
        given_refs.append(refs[len(given_refs)])
        at += given_refs[-1].shape[0]
    came_refs = refs[len(given_refs) : -1]
    half = came_refs[0].shape[1] if came_refs else feat_n
    at = 0
    for given_ref in given_refs:
        rows = pl.ds(at, given_ref.shape[0])
        kept = pl.ds(first + at, given_ref.shape[0])

        def total(columns):
            return keep_ref[kept, columns].astype(F32) + given_ref[:, columns].astype(F32)

        if half == feat_n:
            value = total(pl.ds(0, feat_n))
            for came_ref in came_refs:
                value = value + came_ref[rows, :].astype(F32)
            out_ref[rows, :] = value.astype(BF16)
        else:
            mine = pl.ds(pl.multiple_of(core * half, 128), half)
            other = pl.ds(pl.multiple_of((1 - core) * half, 128), half)
            value = total(mine) + came_refs[0][rows, :].astype(F32)
            out_ref[rows, mine] = value.astype(BF16)
            out_ref[rows, other] = total(other).astype(BF16)
        at += given_ref.shape[0]


def after(value, *others):
    return lax.optimization_barrier((value, *others))[0]


def ring_on_device(grad_out, routes, gate_weights, gate_act, w_down, w_up):
    experts_n = lax.axis_size("ep")
    slot_n = gate_act.shape[1] // experts_n
    token_n = routes.shape[0]
    feat_n = grad_out.shape[1]
    half = feat_n // 2
    unit_n = gate_act.shape[2]
    ring = Ring(experts_n, slot_n, token_n)
    far, pieces = ring.far, ring.pieces
    split = 7 * token_n // 8
    streams = ((0, split), (split, 2 * token_n))
    swap = [(i, i ^ 1) for i in range(experts_n)]
    ring_pairs = ring.pairs()
    core = lax.axis_index("ep") % 2

    def parts_to_core(x, rows):
        return [lax.ppermute(p, "ep", swap) for p in jnp.split(x, x.shape[0] // rows)]

    def streams_to_core(x, *parts):
        return [
            [to_core(x[i:j], j - i) for i, j in zip(range(a, b, n), (*range(a + n, b, n), b))]
            for (a, b), n in zip(streams, parts)
        ]

    def to_core(x, rows=128):
        return jnp.concatenate(parts_to_core(x, rows), axis=0)

    def to_ring(x):
        return lax.ppermute(x, "ep", ring_pairs)

    def to_side(x):
        return lax.ppermute(x, "tp", [(0, 1), (1, 0)])

    def call(kernel, outs, *args, scratch=()):
        return pl.pallas_call(
            kernel,
            out_shape=[jax.ShapeDtypeStruct(shape, BF16) for shape in outs],
            in_specs=[VMEM] * len(args),
            out_specs=[VMEM] * len(outs),
            scratch_shapes=scratch,
            compiler_params=LIMIT,
        )(*args)

    def down(k):
        rows_n = pieces[k] * slot_n
        return call(
            functools.partial(down_kernel, ring, k),
            ([(rows_n, 2 * unit_n)] if k == far else [(rows_n, unit_n)] * 2)
            + [(pieces[k] * token_n, TABLE)],
            *blocks[k],
            w_down[0],
            scratch=[pltpu.VMEM((rows_n, feat_n), BF16)],
        )

    def middle(k, sent):
        hidden = partials[k][0].astype(F32) + sent.astype(F32)
        return (hidden * acts[k].astype(F32)).astype(BF16)

    def up(k, *args):
        shape = (2 * token_n, half) if k == far else (pieces[k] // 2 * token_n, feat_n)
        return call(
            functools.partial(up_kernel, ring, k),
            [shape] * 2,
            partials[k][-1],
            *args,
            w_up[0],
            scratch=[pltpu.VMEM((pieces[k] * slot_n, n), BF16) for n in (2 * unit_n, feat_n)],
        )

    def join(rows, width, *args):
        out = [(rows[1] - rows[0], width)]
        return call(functools.partial(join_kernel, rows[0]), out, *args)[0]

    sibling = to_core(grad_out)
    moving = jnp.concatenate([to_ring(grad_out), to_ring(sibling)], axis=0)
    (table,) = call(table_kernel, [(token_n, TABLE)], routes.T, gate_weights.T)
    tables = [table, to_core(table)]
    blocks = [[jnp.concatenate(x, axis=1) for x in zip([grad_out, sibling], tables)]]
    moving = jnp.concatenate([moving, to_ring(jnp.concatenate(tables, axis=0))], axis=1)
    acts = call(
        functools.partial(act_kernel, ring),
        [(p * slot_n, unit_n) for p in pieces],
        gate_act[0],
    )
    act_peer = to_side(acts[far])
    partials, mines, ups = [down(0)], {}, {}
    sents = [None]
    for k in range(1, far + 1):
        ended = [partials[k - 1][0]] if k > 1 else []
        if k == 2:
            ended += [partials[0][0], act_peer]
        if k < far:
            ended += [acts[0] if k == 1 else sents[k - 1]]
        if k == far - 1:
            ended += [early]
        here = after(moving, *ended)
        if k < far - 1:
            moving = to_ring(here)
        elif k == far - 1:
            part = lax.dynamic_slice_in_dim(here, core * half, half, 1)
            moving = to_ring(jnp.concatenate([part, here[:, feat_n:]], axis=1))
        if k == far - 2:
            mines[k - 1] = middle(k - 1, sents[k - 1])
            early = to_side(mines[k - 1])
            here = after(here, mines[k - 1])
        blocks.append([here, to_core(here, 64 if k == far else 128)])
        if k == far:
            mines[k - 1] = middle(k - 1, sents[k - 1])
            blocks[k][1] = after(blocks[k][1], mines[k - 1])
        partials.append(down(k))
        sents.append(to_side(partials[k][-2]))

    ups[far - 3] = up(far - 3, mines[far - 3], after(early, partials[far][0]))
    swapped = streams_to_core(ups[far - 3][1], 64, 80)
    full = after(sents[far], ups[far - 3][0], *swapped[0], *swapped[1])
    keep, give = up(far, partials[far][0], full, acts[far], act_peer)
    peer = to_side(after(mines[far - 1], full))
    total = join((0, 2 * token_n), half, keep, *parts_to_core(give, 128))
    came = to_ring(total)
    came = [came[a:b] for a, b in streams]
    peer = after(peer, total)
    for k in range(far - 1, 0, -1):
        if k == far - 1:
            mines[k - 1] = middle(k - 1, after(sents[k - 1], peer))
            mines[k] = after(mines[k], mines[k - 1])
        keep, give = ups[k] if k in ups else up(k, mines[k], peer)
        if k == far - 1:
            peer = to_side(mines[k - 1])
        elif k == far - 2:
            mines[0] = middle(0, to_side(after(partials[0][1], peer)))
            peer = to_side(mines[0])
        given = swapped if k in ups else streams_to_core(give, split if k == far - 1 else 64, 2 * token_n - split)
        totals = []
        for i in range(2):
            totals.append(join(streams[i], feat_n, keep, *given[i], came[i]))
            came[i] = to_ring(totals[i])
        came[0] = after(came[0], *totals)
        peer = after(peer, *totals)
    keep, give = up(0, mines[0], peer)
    total = [
        parts_to_core((x.astype(F32) + y.astype(F32)).astype(BF16), x.shape[0])[0]
        for x, y in ((came[0], keep[:split]), (came[1][: token_n - split], keep[split:]))
    ]
    total = jnp.concatenate(total, axis=0).astype(F32)
    return (came[1][token_n - split :].astype(F32) + give.astype(F32) + total).astype(BF16)


def spread_on_device(grad_out, routes, gate_weights, gate_act, w_down, w_up):
    experts_n = lax.axis_size("ep")
    slot_n = gate_act.shape[1] // experts_n
    rows_n = experts_n * slot_n
    token_n, choose_n = routes.shape
    flat_ids = routes.reshape(-1)
    one_hot = (flat_ids[:, None] == jnp.arange(experts_n, dtype=jnp.int32)[None, :]).astype(
        jnp.int32
    )
    earlier = jnp.cumsum(one_hot, axis=0) - one_hot
    slot_rank = jnp.sum(earlier * one_hot, axis=1)
    position = flat_ids * slot_n + slot_rank
    token_ids = jnp.arange(token_n * choose_n, dtype=jnp.int32) // choose_n
    token_of = jnp.full((rows_n,), token_n, jnp.int32).at[position].set(token_ids)
    weight_of = jnp.zeros((rows_n,), jnp.float32).at[position].set(gate_weights.reshape(-1))
    down_local = w_down[0]
    up_local = w_up[0]
    feat_part = grad_out.shape[1]
    padded = jnp.concatenate([grad_out, jnp.zeros((1, feat_part), grad_out.dtype)], axis=0)
    placed = (padded[token_of].astype(jnp.float32) * weight_of[:, None]).astype(jnp.bfloat16)
    placed = placed.reshape(experts_n, slot_n, feat_part)
    partial_value = jnp.einsum(
        "nsd,fd->nsf",
        lax.all_to_all(placed, "ep", split_axis=0, concat_axis=0, tiled=True),
        down_local,
        preferred_element_type=jnp.float32,
    )
    partial_value = partial_value.reshape(rows_n, -1)
    hidden_grad = lax.psum_scatter(
        partial_value.astype(jnp.bfloat16), "tp", scatter_dimension=1, tiled=True
    ).astype(jnp.float32)
    up_grad = (hidden_grad * gate_act[0].astype(jnp.float32)).astype(jnp.bfloat16)
    row_grad = lax.dot_general(
        lax.all_gather(up_grad, "tp", axis=1, tiled=True),
        up_local,
        (((1,), (1,)), ((), ())),
        preferred_element_type=jnp.float32,
    )
    row_grad = row_grad.astype(jnp.bfloat16).reshape(experts_n, slot_n, -1)
    returned = lax.all_to_all(row_grad, "ep", split_axis=0, concat_axis=0, tiled=True)
    picked = returned.reshape(rows_n, -1)[position]
    summed = jnp.sum(picked.astype(jnp.float32).reshape(token_n, choose_n, -1), axis=1)
    return summed.astype(jnp.bfloat16)


def solution(mesh):
    placed = (
        P("ep", "tp"),
        P("ep", None),
        P("ep", None),
        P("ep", None, "tp"),
        P("ep", None, "tp"),
        P("ep", "tp", None),
    )

    def whole(grad_out, routes, *rest):
        ep, tp = mesh.shape["ep"], mesh.shape["tp"]
        dense = tp == 2 and ep % 4 == 0 and 8 <= ep <= 2 * routes.shape[1]
        dense = dense and routes.shape[0] == 128 * ep and grad_out.shape[1] % 512 == 0
        return jax.shard_map(
            ring_on_device if dense else spread_on_device,
            mesh=mesh,
            in_specs=placed,
            out_specs=P("ep", "tp"),
            check_vma=False,
        )(grad_out, routes, *rest)

    return whole
```
